32 devices in a mesh: grp: 2 (over y), head: 2 (over core), seq: 8 (over z, x).
Axes of the slice: x: 2, y: 2, z: 4, core: 2. Of those that a mesh axis runs over, the one named last changes fastest.
Arguments:
- hidden_rows: bfloat16 [2048, 5120], P(('grp', 'seq')), parts along dimension 0, may hold values from -6 to 6
- block_starts: int32 [16], P('grp'), parts along dimension 0, may hold values from 0 to 2944, as said below
- w_qkv: bfloat16 [5120, 3, 5120], P(None, None, ('head', 'seq')), may hold values from -0.078125 to 0.078125
- qk_gain: float32 [2, 5120], P(None, ('head', 'seq')), may hold values from 1.3 to 2.1
- kv_cache: bfloat16 [2, 6144, 5120], P(None, ('grp', 'seq'), 'head'), parts along dimension 1, may hold values from -92 to 92
- w_out: bfloat16 [5120, 5120], P('head', 'seq'), may hold values from -0.078125 to 0.078125
Outputs:
- mixed: bfloat16 [2048, 5120], P(('grp', 'head'), 'seq'), parts along dimension 0
The draws below stay inside these ranges and needn't reach their ends.
There are 2 independent parts, one for each index of `grp`. The reference program is written for one: setup_inputs(seed, part) draws one part's arguments, and reference() takes and returns one part's arrays. A program takes and returns all parts, laid end to end along the dimension named above; an argument that names none is the same for every part. Nothing has to cross between parts.
Inputs may be any that keep to these rules, and one draw needn't show every extreme that they name: `block_starts`: all different, each a multiple of 128.
All inputs are finite; a program needn't handle non-finite values.
Results may differ from the reference program's by a relative error of at most 0.03.
Values may be sent and summed in bfloat16 or wider, within the bound.
A program may use at most 128 MiB of HBM per device.

```python
import jax
import jax.numpy as jnp
from jax import lax

D = 5120
HEADS = 40
HD = 128
BLK = 128
NBLK = 8
CH = 1024
SEQLEN = 3072


def draw_block_starts(key, part):
    key = jax.random.fold_in(key, 11)
    order = jax.random.permutation(key, SEQLEN // BLK)
    return (order[:NBLK] * BLK).astype(jnp.int32)


def draw_kv_cache(key, part):
    key = jax.random.fold_in(key, 7)
    first, second = jax.random.split(key, 2)
    width = HEADS * HD
    lifted = jnp.clip(jax.random.normal(first, (SEQLEN, width), jnp.float32), -6.0, 6.0) * 1.75
    values = jnp.clip(jax.random.normal(second, (SEQLEN, width), jnp.float32), -6.0, 6.0)
    return jnp.stack([lifted, values]).astype(jnp.bfloat16)


def block_levels(stream_key, extent, shards, low, top_value):
    loudness, own = 1.0, jax.random.fold_in(stream_key, 6)
    for position, parts in shards:
        steps = jnp.exp(jax.random.uniform(jax.random.fold_in(own, position), (parts,), jnp.float32, low / len(shards), top_value / len(shards)))
        loudness = loudness * jnp.repeat(steps, extent[position] // parts).reshape([-1 if axis == position else 1 for axis in range(len(extent))])
    return loudness


def gaussian(rng, extent, scale, most, cuts=(), kind=jnp.bfloat16):
    level = block_levels(rng, extent, cuts, -0.22, 0.18) if cuts else 1.0
    result = jax.random.normal(rng, extent, jnp.float32) * scale * level
    return jnp.minimum(jnp.maximum(result, -most), most).astype(kind)


def setup_inputs(seed: int = 0, part: int = 0) -> dict:
    arg_keys = jax.random.split(jax.random.key(seed), 7)
    part_keys = jax.random.split(jax.random.fold_in(arg_keys[6], part), 7)
    return {
        "hidden_rows": gaussian(part_keys[0], (CH, D), 1.0, 6.0, ((0, 8),)),
        "block_starts": draw_block_starts(jax.random.fold_in(jax.random.fold_in(arg_keys[6], part), 71), part),
        "w_qkv": gaussian(arg_keys[2], (D, 3, HEADS * HD), D ** -0.5, 0.078125, ((2, 16),)),
        "qk_gain": jnp.clip(1.3 + 0.79999995 * jax.random.uniform(arg_keys[3], (2, HEADS * HD), jnp.float32) ** block_levels(arg_keys[3], (2, HEADS * HD), ((1, 16),), -0.2, 0.2), 1.3, 2.1),
        "kv_cache": draw_kv_cache(jax.random.fold_in(jax.random.fold_in(arg_keys[6], part), 71), part),
        "w_out": gaussian(arg_keys[5], (HEADS * HD, D), (HEADS * HD) ** -0.5, 0.078125, ((0, 2), (1, 8))),
    }


def reference(hidden_rows, block_starts, w_qkv, qk_gain, kv_cache, w_out):
    width = HEADS * HD
    projected = jnp.dot(hidden_rows, w_qkv.reshape(D, 3 * width), preferred_element_type=jnp.float32).reshape(CH, 3, width)
    paired = projected[:, :2]
    mean_sq = lax.optimization_barrier(jnp.sum(paired * paired, axis=2, keepdims=True)) / width
    normed = paired * lax.rsqrt(mean_sq + 1e-06) * qk_gain[None]
    fresh = jnp.concatenate([normed, projected[:, 2:]], axis=1).astype(jnp.bfloat16)
    offsets = jnp.arange(BLK, dtype=jnp.int32)
    positions = (block_starts[:, None].astype(jnp.int32) + offsets[None]).reshape(CH)
    keys = kv_cache[0].at[positions].set(fresh[:, 1])
    values = kv_cache[1].at[positions].set(fresh[:, 2])
    query = fresh[:, 0]

    def one_head(index):
        start = index * HD
        head_q = lax.dynamic_slice_in_dim(query, start, HD, 1)
        head_k = lax.dynamic_slice_in_dim(keys, start, HD, 1)
        head_v = lax.dynamic_slice_in_dim(values, start, HD, 1)
        scores = jnp.dot(head_q, head_k.T, preferred_element_type=jnp.float32) * HD ** (-0.5)
        top = lax.optimization_barrier(jnp.max(scores, axis=1, keepdims=True))
        weights = jnp.exp(scores - top)
        total = lax.optimization_barrier(jnp.sum(weights, axis=1, keepdims=True))
        probs = weights.astype(jnp.bfloat16)
        return jnp.dot(probs, head_v, preferred_element_type=jnp.float32) / total
    per_head = lax.map(one_head, jnp.arange(HEADS, dtype=jnp.int32))
    attended = jnp.transpose(per_head, (1, 0, 2)).reshape(CH, width).astype(jnp.bfloat16)
    return jnp.dot(attended, w_out, preferred_element_type=jnp.float32).astype(jnp.bfloat16)
```

```python
import functools

import jax
import jax.numpy as jnp
from jax import lax
from jax.experimental import pallas as pl
from jax.experimental.pallas import tpu as pltpu
from jax.sharding import PartitionSpec as P

HEADS = 40
HD = 128
BLK = 128
NBLK = 8
PAIR = 2
TILE = 256
MESH = pl.DeviceIdType.MESH
VMEM_LIMIT = 56 * 1024 * 1024


def remote(src, dst, send, recv, where):
    return pltpu.make_async_remote_copy(
        src_ref=src, dst_ref=dst, send_sem=send, recv_sem=recv, device_id=where, device_id_type=MESH
    )


def exchange_kernel(
    count, hidden_ref, cache_ref, full_ref, spread_ref,
    recv_sem, up_sem, down_sem, side_sem, core_sem, kv_send, kv_recv, own_sem,
):
    me = lax.axis_index("seq")
    core = lax.axis_index("head")
    line = count // PAIR
    z, x = me // PAIR, me % PAIR
    rows = hidden_ref.shape[0]
    half = rows // 2
    length = cache_ref.shape[1]
    group = cache_ref.shape[2] // line
    above, below = {"seq": me + PAIR}, {"seq": me - PAIR}
    partner = {"seq": z * PAIR + 1 - x}
    other = {"head": 1 - core}

    barrier = pltpu.get_barrier_semaphore()
    for step in range(1, count):
        pl.semaphore_signal(barrier, inc=1, device_id={"seq": lax.rem(me + step, count)}, device_id_type=MESH)
    pl.semaphore_signal(barrier, inc=1, device_id=other, device_id_type=MESH)
    pl.semaphore_wait(barrier, count)

    def place(owner, part):
        return full_ref.at[pl.ds(pl.multiple_of(owner * rows + part * half, half), half), :]

    mine = hidden_ref.at[pl.ds(pl.multiple_of(core * half, half), half), :]

    def relay(owner, part, sem, where, src=None):
        spot = place(owner, part)
        return remote(spot if src is None else src, spot, sem, recv_sem.at[owner * 2 + part], where)

    @pl.when(z < line - 1)
    def _():
        relay(me, core, up_sem.at[0], above, mine).start()

    @pl.when(z > 0)
    def _():
        relay(me, core, down_sem.at[0], below, mine).start()

    relay(me, core, side_sem.at[line - 1], partner, mine).start()
    own = pltpu.make_async_copy(
        hidden_ref, full_ref.at[pl.ds(pl.multiple_of(me * rows, rows), rows), :], own_sem.at[0]
    )
    own.start()

    def pieces(owner):
        to_z, to_x = owner // PAIR, owner % PAIR
        pair_at = pl.multiple_of(to_z * group + to_x * 3 * HD, HD)
        middle_at = pl.multiple_of(to_z * group + 2 * HD, HD)
        return (
            cache_ref.at[:, :, pl.ds(pair_at, 2 * HD)],
            cache_ref.at[:, :, pl.ds(middle_at, HD)],
        )

    def slots(owner):
        at = pl.ds(pl.multiple_of(owner * length, length), length)
        return spread_ref.at[:, at, pl.ds(0, 2 * HD)], spread_ref.at[:, at, pl.ds(2 * HD, HD)]

    locals_ = [
        pltpu.make_async_copy(src, dst, own_sem.at[1 + i])
        for i, (src, dst) in enumerate(zip(pieces(me), slots(me)))
    ]
    sends = []
    for step in range(1, count):
        to = lax.rem(me + step, count)
        for i, (src, dst) in enumerate(zip(pieces(to), slots(me))):
            sends.append(remote(src, dst, kv_send.at[2 * step + i], kv_recv.at[2 * step + i], {"seq": to}))
    for copy in locals_ + sends:
        copy.start()

    def arrived(owner, part):
        relay(owner, part, core_sem.at[0], other).wait_recv()

    def handle_low(d):
        @pl.when(z - d >= 0)
        def _():
            owner = me - d * PAIR
            arrived(owner, core)

            @pl.when(z < line - 1)
            def _():
                relay(owner, core, up_sem.at[d], above).start()

            relay(owner, core, side_sem.at[line - 1 - d], partner).start()
            relay(owner, core, core_sem.at[line - 1 - d], other).start()

    def handle_high(d):
        @pl.when(z + d < line)
        def _():
            owner = me + d * PAIR
            arrived(owner, core)

            @pl.when(z > 0)
            def _():
                relay(owner, core, down_sem.at[d], below).start()

            relay(owner, core, side_sem.at[line - 1 + d], partner).start()
            relay(owner, core, core_sem.at[line - 1 + d], other).start()

    def handle_side(d):
        @pl.when(jnp.logical_and(z + d >= 0, z + d < line))
        def _():
            owner = (z + d) * PAIR + 1 - x
            arrived(owner, core)
            relay(owner, core, core_sem.at[2 * line - 1 + line - 1 + d], other).start()

    for d in range(line):
        if d + 1 < line:
            handle_low(d + 1)
            handle_high(d + 1)
        handle_side(d)
        if d:
            handle_side(-d)

    own.wait()
    for step in range(1, count):
        arrived(lax.rem(me + step, count), 1 - core)

    def sent(owner, sem, where):
        relay(owner, core, sem, where).wait_send()

    for d in range(line):
        @pl.when(jnp.logical_and(z < line - 1, z - d >= 0))
        def _():
            sent(me, up_sem.at[d], above)

        @pl.when(jnp.logical_and(z > 0, z + d < line))
        def _():
            sent(me, down_sem.at[d], below)

    for d in range(1 - line, line):
        @pl.when(jnp.logical_and(z + d >= 0, z + d < line))
        def _():
            sent(me, side_sem.at[line - 1 + d], partner)
            if d:
                sent(me, core_sem.at[line - 1 + d], other)
            sent(me, core_sem.at[2 * line - 1 + line - 1 + d], other)

    for copy in locals_:
        copy.wait()
    for copy in sends:
        copy.wait()


def exchange(hidden_rows, kv_cache, count):
    rows, width = hidden_rows.shape
    line = count // PAIR
    dma = pltpu.SemaphoreType.DMA
    return pl.pallas_call(
        functools.partial(exchange_kernel, count),
        out_shape=(
            jax.ShapeDtypeStruct((rows * count, width), hidden_rows.dtype),
            jax.ShapeDtypeStruct((2, kv_cache.shape[1] * count, 3 * HD), kv_cache.dtype),
        ),
        in_specs=[pl.BlockSpec(memory_space=pl.ANY)] * 2,
        out_specs=[pl.BlockSpec(memory_space=pl.ANY)] * 2,
        scratch_shapes=[
            dma((2 * count,)), dma((line,)), dma((line,)), dma((2 * line - 1,)),
            dma((2 * (2 * line - 1),)), dma((2 * count,)), dma((2 * count,)), dma((3,)),
        ],
        compiler_params=pltpu.CompilerParams(
            collective_id=0, has_side_effects=True, vmem_limit_bytes=VMEM_LIMIT
        ),
    )(hidden_rows, kv_cache)


def attend_kernel(starts_ref, side_ref, query_ref, cache_ref, newer_ref, pair_ref, middle_ref, held):
    step = pl.program_id(0)

    @pl.when(step % 4 == 0)
    def _():
        held[...] = cache_ref[...]
        for number in range(NBLK):
            at = pl.multiple_of(starts_ref[number], BLK)
            held[:, pl.ds(at, BLK), :] = newer_ref[:, number * BLK : (number + 1) * BLK, :]

    scores = lax.dot_general(
        query_ref[...], held[0], (((1,), (1,)), ((), ())), preferred_element_type=jnp.float32
    )
    top = jnp.max(scores, axis=1, keepdims=True)
    weights = jnp.exp((scores - top) * HD ** (-0.5))
    total = jnp.sum(weights, axis=1, keepdims=True)
    summed = jnp.dot(weights.astype(jnp.bfloat16), held[1], preferred_element_type=jnp.float32)
    result = (summed / total).astype(jnp.bfloat16)

    @pl.when(step < 8)
    def _():
        pair_ref[...] = result

    @pl.when(step >= 8)
    def _():
        middle_ref[...] = result


def attend(block_starts, side, query, spread, newer):
    rows = query.shape[0]
    positions = spread.shape[1]
    tiles = rows // TILE

    def query_at(u, starts, side):
        inner = jnp.where(u < 2 * tiles, u % tiles, side[0] * (tiles // 2) + u - 2 * tiles)
        return inner, u // tiles

    def pair_at(u, starts, side):
        v = jnp.minimum(u, 2 * tiles - 1)
        return v % tiles, v // tiles

    return pl.pallas_call(
        attend_kernel,
        out_shape=(
            jax.ShapeDtypeStruct((rows, 2 * HD), jnp.bfloat16),
            jax.ShapeDtypeStruct((rows // 2, HD), jnp.bfloat16),
        ),
        grid_spec=pltpu.PrefetchScalarGridSpec(
            num_scalar_prefetch=2,
            grid=(2 * tiles + tiles // 2,),
            in_specs=[
                pl.BlockSpec((TILE, HD), query_at),
                pl.BlockSpec((2, positions, HD), lambda u, starts, side: (0, 0, u // tiles)),
                pl.BlockSpec((2, rows, HD), lambda u, starts, side: (0, 0, u // tiles)),
            ],
            out_specs=[
                pl.BlockSpec((TILE, HD), pair_at),
                pl.BlockSpec((TILE, HD), lambda u, starts, side: (jnp.maximum(u - 2 * tiles, 0), 0)),
            ],
            scratch_shapes=[pltpu.VMEM((2, positions, HD), jnp.bfloat16)],
        ),
        compiler_params=pltpu.CompilerParams(vmem_limit_bytes=VMEM_LIMIT),
    )(block_starts, side, query, spread, newer)


def collect_kernel(count, pair_ref, middle_ref, full_ref, recv_sem, up_sem, down_sem, side_sem, own_sem):
    me = lax.axis_index("seq")
    line = count // PAIR
    z, x = me // PAIR, me % PAIR
    rows = pair_ref.shape[0]
    group = full_ref.shape[1] // line
    above, below = {"seq": me + PAIR}, {"seq": me - PAIR}
    partner = {"seq": z * PAIR + 1 - x}

    barrier = pltpu.get_barrier_semaphore()

    def greet(where):
        pl.semaphore_signal(barrier, inc=1, device_id=where, device_id_type=MESH)

    @pl.when(z < line - 1)
    def _():
        greet(above)

    @pl.when(z > 0)
    def _():
        greet(below)

    greet(partner)
    neighbours = 1 + (z < line - 1).astype(jnp.int32) + (z > 0).astype(jnp.int32)
    pl.semaphore_wait(barrier, neighbours)

    def spots(owner):
        to_z, to_x = owner // PAIR, owner % PAIR
        pair_at = pl.multiple_of(to_z * group + to_x * 3 * HD, HD)
        middle_at = pl.multiple_of(to_z * group + 2 * HD, HD)
        low = pl.multiple_of(to_x * (rows // 2), rows // 2)
        return (
            full_ref.at[:, pl.ds(pair_at, 2 * HD)],
            full_ref.at[pl.ds(low, rows // 2), pl.ds(middle_at, HD)],
        )

    own_blocks = (pair_ref, middle_ref)

    def relay(owner, sem, at, where, first=False):
        return [
            remote(own_blocks[i] if first else spot, spot, sem.at[2 * at + i], recv_sem.at[2 * owner + i], where)
            for i, spot in enumerate(spots(owner))
        ]

    def start(*args):
        for copy in relay(*args):
            copy.start()

    def arrived(owner):
        for copy in relay(owner, side_sem, 0, partner):
            copy.wait_recv()

    def sent(sem, at, where):
        for copy in relay(me, sem, at, where):
            copy.wait_send()

    @pl.when(z < line - 1)
    def _():
        start(me, up_sem, 0, above, True)

    @pl.when(z > 0)
    def _():
        start(me, down_sem, 0, below, True)

    start(me, side_sem, line - 1, partner, True)
    own = [
        pltpu.make_async_copy(block, spot, own_sem.at[i])
        for i, (block, spot) in enumerate(zip(own_blocks, spots(me)))
    ]
    for copy in own:
        copy.start()

    def handle_low(d):
        @pl.when(z - d >= 0)
        def _():
            owner = me - d * PAIR
            arrived(owner)

            @pl.when(z < line - 1)
            def _():
                start(owner, up_sem, d, above)

            start(owner, side_sem, line - 1 - d, partner)

    def handle_high(d):
        @pl.when(z + d < line)
        def _():
            owner = me + d * PAIR
            arrived(owner)

            @pl.when(z > 0)
            def _():
                start(owner, down_sem, d, below)

            start(owner, side_sem, line - 1 + d, partner)

    for d in range(1, line):
        handle_low(d)
        handle_high(d)
    for copy in own:
        copy.wait()

    for d in range(1 - line, line):
        @pl.when(jnp.logical_and(z + d >= 0, z + d < line))
        def _():
            arrived((z + d) * PAIR + 1 - x)
            sent(side_sem, line - 1 + d, partner)

    for d in range(line):
        @pl.when(jnp.logical_and(z < line - 1, z - d >= 0))
        def _():
            sent(up_sem, d, above)

        @pl.when(jnp.logical_and(z > 0, z + d < line))
        def _():
            sent(down_sem, d, below)


def collect(pair, middle, count, width):
    line = count // PAIR
    dma = pltpu.SemaphoreType.DMA
    return pl.pallas_call(
        functools.partial(collect_kernel, count),
        out_shape=jax.ShapeDtypeStruct((pair.shape[0], width), pair.dtype),
        in_specs=[pl.BlockSpec(memory_space=pl.ANY)] * 2,
        out_specs=pl.BlockSpec(memory_space=pl.ANY),
        scratch_shapes=[
            dma((2 * count,)), dma((2 * line,)), dma((2 * line,)), dma((2 * (2 * line - 1),)), dma((2,)),
        ],
        compiler_params=pltpu.CompilerParams(
            collective_id=1, has_side_effects=True, vmem_limit_bytes=VMEM_LIMIT
        ),
    )(pair, middle)


def by_heads(hidden_rows, block_starts, w_qkv, qk_gain, kv_cache, w_out):
    count = lax.axis_size("seq")
    side = lax.axis_index("seq") % PAIR
    columns = w_qkv.shape[2]
    features = kv_cache.shape[2]
    full, spread = exchange(hidden_rows, kv_cache, count)
    rows = full.shape[0]
    flat_w = w_qkv.reshape(w_qkv.shape[0], 3 * columns)
    projected = jnp.dot(full, flat_w, preferred_element_type=jnp.float32).reshape(rows, 3, columns)
    projected = jnp.transpose(projected, (1, 0, 2))
    paired = projected[:2]
    squares = jnp.sum(paired * paired, axis=2)
    totals = lax.psum(squares, ("head", "seq"))
    factor = lax.rsqrt(totals / (HEADS * HD) + 1e-06)
    normed = paired * factor[:, :, None] * qk_gain[:, None, :]
    fresh = jnp.concatenate([normed, projected[2:]], axis=0).astype(jnp.bfloat16)
    part = HD // 2
    give = jnp.where(side == 0, fresh[:, :, columns - part :], fresh[:, :, :part])
    route = [(i, i + 1 - 2 * (i % PAIR)) for i in range(count)]
    taken = lax.ppermute(give, "seq", route)
    heads = jnp.where(
        side == 0,
        jnp.concatenate([fresh, taken], axis=2),
        jnp.concatenate([fresh[:, :, part:], taken, fresh[:, :, :part]], axis=2),
    )
    pair, middle = attend(
        block_starts, side.reshape(1).astype(jnp.int32), heads[0], spread, heads[1:]
    )
    gathered = collect(pair, middle, count, features)
    return lax.psum_scatter(
        jnp.dot(gathered, w_out, preferred_element_type=jnp.float32).astype(jnp.bfloat16),
        "head",
        scatter_dimension=0,
        tiled=True,
    )


def shifted(block, axis, distance):
    devices = range(lax.axis_size(axis))
    route = [((i - distance) % len(devices), i) for i in devices]
    return lax.ppermute(block, axis, route)


def write_blocks(kv_cache, newer, block_starts):
    length = kv_cache.shape[1]
    first = lax.axis_index("seq") * length
    cache = kv_cache
    for number in range(NBLK):
        offset = block_starts[number] - first
        inside = jnp.logical_and(offset >= 0, offset < length)
        place = jnp.clip(offset, 0, length - BLK)
        block = jnp.transpose(newer[number * BLK : (number + 1) * BLK], (1, 0, 2))
        present = lax.dynamic_slice_in_dim(cache, place, BLK, 1)
        cache = lax.dynamic_update_slice_in_dim(cache, jnp.where(inside, block, present), place, 1)
    return cache


def by_positions(hidden_rows, block_starts, w_qkv, qk_gain, kv_cache, w_out):
    columns = w_qkv.shape[2]
    flat_w = w_qkv.reshape(w_qkv.shape[0], 3 * columns)
    piece = lax.all_gather(hidden_rows, "seq", axis=0, tiled=True)
    projected = jnp.dot(piece, flat_w, preferred_element_type=jnp.float32).reshape(
        piece.shape[0], 3, columns
    )
    paired = projected[:, :2]
    squares = jnp.sum(paired * paired, axis=2)
    totals = lax.psum(squares, ("head", "seq"))
    factor = lax.rsqrt(totals / (HEADS * HD) + 1e-06)
    normed = paired * factor[:, :, None] * qk_gain[None]
    fresh = jnp.concatenate([normed, projected[:, 2:]], axis=1).astype(jnp.bfloat16)
    features = kv_cache.shape[2]
    heads = features // HD
    length = kv_cache.shape[1]
    own = lax.all_to_all(fresh, "seq", split_axis=0, concat_axis=2, tiled=True)
    newer = lax.all_gather(own[:, 1:], "seq", axis=0, tiled=True)
    cache = write_blocks(kv_cache, newer, block_starts)
    keys = cache[0].reshape(length, heads, HD)
    values = cache[1].reshape(length, heads, HD)
    rows = own.shape[0]
    query_rows = own[:, 0].reshape(rows, heads, HD)
    start_state = (
        query_rows,
        jnp.full((rows, heads), -1e30, jnp.float32),
        jnp.zeros((rows, heads), jnp.float32),
        jnp.zeros((rows, heads, HD), jnp.float32),
    )

    def visit(step, state):
        query_now, top_old, total_old, summed_old = state
        scores = jnp.einsum(
            "rhd,thd->hrt", query_now, keys, preferred_element_type=jnp.float32
        ) * HD ** (-0.5)
        top_new = jnp.maximum(top_old, jnp.max(scores, axis=2).T)
        weights = jnp.exp(scores - top_new.T[:, :, None])
        decay = jnp.exp(top_old - top_new)
        total_new = total_old * decay + jnp.sum(weights, axis=2).T
        summed_new = summed_old * decay[:, :, None] + jnp.einsum(
            "hrt,thd->rhd", weights.astype(jnp.bfloat16), values, preferred_element_type=jnp.float32
        )
        return (
            shifted(query_now, "seq", 1),
            shifted(top_new.astype(jnp.bfloat16), "seq", 1).astype(top_new.dtype),
            shifted(total_new.astype(jnp.bfloat16), "seq", 1).astype(total_new.dtype),
            shifted(summed_new.astype(jnp.bfloat16), "seq", 1).astype(summed_new.dtype),
        )

    final = lax.fori_loop(0, lax.axis_size("seq"), visit, start_state)
    summed = final[3]
    total = final[2]
    attended = (summed / total[:, :, None]).astype(jnp.bfloat16).reshape(summed.shape[0], features)
    gathered = lax.all_gather(attended, "seq", axis=0, tiled=True)
    result = lax.psum_scatter(
        jnp.dot(gathered, w_out, preferred_element_type=jnp.float32).astype(jnp.bfloat16),
        "head",
        scatter_dimension=0,
        tiled=True,
    )
    return result


def solution(mesh):
    count = mesh.shape["seq"]
    split = mesh.shape["head"] * count
    fits = mesh.shape["head"] == 2 and count % PAIR == 0 and HEADS * PAIR == 5 * split
    return jax.shard_map(
        by_heads if fits else by_positions,
        mesh=mesh,
        in_specs=(
            P(("grp", "seq"), None),
            P("grp"),
            P(None, None, ("head", "seq")),
            P(None, ("head", "seq")),
            P(None, ("grp", "seq"), "head"),
            P("head", "seq"),
        ),
        out_specs=P(("grp", "head"), "seq"),
        check_vma=False,
    )
```

```python
import functools

import jax
import jax.numpy as jnp
from jax import lax
from jax.experimental import pallas as pl
from jax.experimental.pallas import tpu as pltpu
from jax.sharding import PartitionSpec as P

HEADS = 40
HD = 128
BLK = 128
NBLK = 8
PAIR = 2
TILE = 256
MESH = pl.DeviceIdType.MESH
VMEM_LIMIT = 56 * 1024 * 1024


def remote(src, dst, send, recv, where):
    return pltpu.make_async_remote_copy(
        src_ref=src, dst_ref=dst, send_sem=send, recv_sem=recv, device_id=where, device_id_type=MESH
    )


def exchange_kernel(
    count, hidden_ref, weight_ref, gain_ref, cache_ref, fresh_ref, spread_ref,
    full, pair_w, middle_w, projected, shared, mine_mid, theirs_mid, sums,
    recv_sem, up_sem, down_sem, side_sem, core_sem, kv_send, kv_recv, own_sem,
    sum_send, sum_recv, pass_send, pass_recv, mid_sem,
):
    me = lax.axis_index("seq")
    core = lax.axis_index("head")
    line = count // PAIR
    z, x = me // PAIR, me % PAIR
    rows = hidden_ref.shape[0]
    half = rows // 2
    length = cache_ref.shape[1]
    group = cache_ref.shape[2] // line
    columns = weight_ref.shape[0] // 3
    own_part = columns - 2 * HD
    above, below = {"seq": me + PAIR}, {"seq": me - PAIR}
    partner_at = z * PAIR + 1 - x
    partner = {"seq": partner_at}
    other = {"head": 1 - core}
    peers = [
        (lax.rem(core + c, 2), lax.rem(me + step, count))
        for c in range(2)
        for step in range(count)
        if c or step
    ]

    barrier = pltpu.get_barrier_semaphore()
    for to_core, to in peers:
        pl.semaphore_signal(barrier, inc=1, device_id={"head": to_core, "seq": to}, device_id_type=MESH)
    pl.semaphore_wait(barrier, 2 * count - 1)

    def place(owner, part):
        return full.at[pl.ds(pl.multiple_of(owner * rows + part * half, half), half), :]

    mine = hidden_ref.at[pl.ds(pl.multiple_of(core * half, half), half), :]

    def relay(owner, part, sem, where, src=None):
        spot = place(owner, part)
        return remote(spot if src is None else src, spot, sem, recv_sem.at[owner * 2 + part], where)

    @pl.when(z < line - 1)
    def _():
        relay(me, core, up_sem.at[0], above, mine).start()

    @pl.when(z > 0)
    def _():
        relay(me, core, down_sem.at[0], below, mine).start()

    relay(me, core, side_sem.at[line - 1], partner, mine).start()
    loads = [
        pltpu.make_async_copy(
            hidden_ref, full.at[pl.ds(pl.multiple_of(me * rows, rows), rows), :], own_sem.at[0]
        )
    ]
    for c in range(3):
        pair_at = pl.multiple_of(c * columns + x * own_part, 16)
        middle_at = pl.multiple_of(c * columns + (1 - x) * 2 * HD, 16)
        into = pl.multiple_of(c * HD + x * own_part, 16)
        away = pl.multiple_of(c * HD + (1 - x) * own_part, 16)
        loads.append(
            pltpu.make_async_copy(
                weight_ref.at[pl.ds(pair_at, 2 * HD), :], pair_w.at[pl.ds(c * 2 * HD, 2 * HD), :], own_sem.at[1 + c]
            )
        )
        loads.append(
            pltpu.make_async_copy(
                weight_ref.at[pl.ds(middle_at, own_part), :], middle_w.at[pl.ds(into, own_part), :], own_sem.at[4 + c]
            )
        )
        middle_w[pl.ds(away, own_part), :] = jnp.zeros((own_part, middle_w.shape[1]), middle_w.dtype)
    for copy in loads:
        copy.start()

    def arrived(owner, part):
        relay(owner, part, core_sem.at[0], other).wait_recv()

    def handle_low(d):
        @pl.when(z - d >= 0)
        def _():
            owner = me - d * PAIR
            arrived(owner, core)

            @pl.when(z < line - 1)
            def _():
                relay(owner, core, up_sem.at[d], above).start()

            relay(owner, core, side_sem.at[line - 1 - d], partner).start()
            relay(owner, core, core_sem.at[line - 1 - d], other).start()

    def handle_high(d):
        @pl.when(z + d < line)
        def _():
            owner = me + d * PAIR
            arrived(owner, core)

            @pl.when(z > 0)
            def _():
                relay(owner, core, down_sem.at[d], below).start()

            relay(owner, core, side_sem.at[line - 1 + d], partner).start()
            relay(owner, core, core_sem.at[line - 1 + d], other).start()

    def handle_side(d):
        @pl.when(jnp.logical_and(z + d >= 0, z + d < line))
        def _():
            owner = (z + d) * PAIR + 1 - x
            arrived(owner, core)
            relay(owner, core, core_sem.at[2 * line - 1 + line - 1 + d], other).start()

    def source(owner):
        return owner // PAIR, owner % PAIR

    def pair_copy(step, to):
        to_z, to_x = source(to)
        at = pl.multiple_of(to_z * group + to_x * 3 * HD, HD)
        src = cache_ref.at[:, :, pl.ds(at, 2 * HD)]
        dst = spread_ref.at[:, pl.ds(pl.multiple_of(me * length, length), length), pl.ds(0, 2 * HD)]
        return src, dst

    part = length // 2

    def middle_slot(owner, which):
        at = pl.multiple_of(owner * length + which * part, part)
        return spread_ref.at[:, pl.ds(at, part), pl.ds(2 * HD, HD)]

    def middle_copy(to):
        to_z, to_x = source(to)
        at = pl.multiple_of(to_z * group + 2 * HD, HD)
        low = pl.multiple_of(to_x * part, part)
        return cache_ref.at[:, pl.ds(low, part), pl.ds(at, HD)], middle_slot(me, to_x)

    middle_at = pl.multiple_of(z * group + 2 * HD, HD)
    whole_middle = (
        cache_ref.at[:, :, pl.ds(middle_at, HD)],
        spread_ref.at[:, pl.ds(pl.multiple_of(me * length, length), length), pl.ds(2 * HD, HD)],
    )
    locals_ = [
        pltpu.make_async_copy(*pair_copy(0, me), own_sem.at[7]),
        pltpu.make_async_copy(*whole_middle, own_sem.at[8]),
    ]
    far = []
    for hop in range(1, line):
        for across in range(PAIR):
            to = lax.rem(z + hop, line) * PAIR + lax.rem(x + across, PAIR)
            far.append((hop * PAIR + across, to, lax.rem(z + line - hop, line) * PAIR + lax.rem(x + across, PAIR)))
    sends = []
    for slot, to, _ in far:
        sends.append(remote(*middle_copy(to), kv_send.at[2 * slot], kv_recv.at[2 * slot], {"seq": to}))
    sends.append(remote(*whole_middle, kv_send.at[0], kv_recv.at[0], partner))
    for slot, to, _ in far:
        sends.append(remote(*pair_copy(slot, to), kv_send.at[2 * slot + 1], kv_recv.at[2 * slot + 1], {"seq": to}))
    sends.append(remote(*pair_copy(0, partner_at), kv_send.at[1], kv_recv.at[1], partner))

    for d in range(line):
        if d + 1 < line:
            handle_low(d + 1)
            handle_high(d + 1)
        if d + 1 == max(line - 2, 1):
            for copy in sends + locals_:
                copy.start()
        handle_side(d)
        if d:
            handle_side(-d)

    for copy in loads:
        copy.wait()
    for step in range(1, count):
        arrived(lax.rem(me + step, count), 1 - core)

    tile = 2 * HD
    tiles = full.shape[0] // tile
    nt = (((1,), (1,)), ((), ()))

    @pl.loop(0, tiles)
    def _(t):
        at = pl.ds(pl.multiple_of(t * tile, tile), tile)
        lines = full[at, :]
        for c in range(3):
            wide = lax.dot_general(
                lines, pair_w[c * 2 * HD : (c + 1) * 2 * HD, :], nt, preferred_element_type=jnp.float32
            )
            thin = lax.dot_general(
                lines, middle_w[c * HD : (c + 1) * HD, :], nt, preferred_element_type=jnp.float32
            )
            if c == 2:
                fresh_ref[2, at, 0 : 2 * HD] = wide.astype(jnp.bfloat16)
                mine_mid[2, at, :] = thin.astype(jnp.bfloat16)
            else:
                projected[c, at, 0 : 2 * HD] = wide
                projected[c, at, 2 * HD : 3 * HD] = thin
                square = jnp.sum(wide * wide, axis=1, keepdims=True) + jnp.sum(thin * thin, axis=1, keepdims=True)
                turned = jnp.transpose(jnp.broadcast_to(square, (tile, HD)))
                sums[0, pl.ds(c * tiles + t, 1), :] = turned[0:1, :]

    shares = []
    for i, (to_core, to) in enumerate(peers):
        shares.append(
            remote(
                sums.at[0], sums.at[i + 1], sum_send.at[i], sum_recv.at[i], {"head": to_core, "seq": to}
            )
        )
    for copy in shares:
        copy.start()
    for copy in shares:
        copy.wait()
    total = sums[0]
    for i in range(1, 2 * count):
        total = total + sums[i]
    shared[...] = lax.rsqrt(total / (HEADS * HD) + 1e-06)

    @pl.loop(0, tiles)
    def _(t):
        at = pl.ds(pl.multiple_of(t * tile, tile), tile)
        for c in range(2):
            factor = jnp.transpose(jnp.broadcast_to(shared[pl.ds(c * tiles + t, 1), :], (HD, tile)))
            for k in range(3):
                lanes = slice(k * HD, (k + 1) * HD)
                normed = (projected[c, at, lanes] * factor * gain_ref[c : c + 1, lanes]).astype(jnp.bfloat16)
                if k < 2:
                    fresh_ref[c, at, lanes] = normed
                else:
                    mine_mid[c, at, :] = normed

    swap = remote(mine_mid, theirs_mid, mid_sem.at[0], mid_sem.at[1], partner)
    swap.start()

    passes = []
    for slot, to, owner in far:
        remote(*middle_copy(to), kv_send.at[2 * slot], kv_recv.at[2 * slot], {"seq": to}).wait_recv()
        spot = middle_slot(owner, x)
        copy = remote(spot, spot, pass_send.at[slot], pass_recv.at[slot], partner)
        copy.start()
        passes.append(copy)

    swap.wait()

    @pl.loop(0, tiles)
    def _(t):
        at = pl.ds(pl.multiple_of(t * tile, tile), tile)
        for c in range(3):
            fresh_ref[c, at, 2 * HD : 3 * HD] = mine_mid[c, at, :] + theirs_mid[c, at, :]

    def sent(owner, sem, where):
        relay(owner, core, sem, where).wait_send()

    for d in range(line):
        @pl.when(jnp.logical_and(z < line - 1, z - d >= 0))
        def _():
            sent(me, up_sem.at[d], above)

        @pl.when(jnp.logical_and(z > 0, z + d < line))
        def _():
            sent(me, down_sem.at[d], below)

    for d in range(1 - line, line):
        @pl.when(jnp.logical_and(z + d >= 0, z + d < line))
        def _():
            sent(me, side_sem.at[line - 1 + d], partner)
            if d:
                sent(me, core_sem.at[line - 1 + d], other)
            sent(me, core_sem.at[2 * line - 1 + line - 1 + d], other)

    for copy in locals_:
        copy.wait()
    for i, copy in enumerate(sends):
        copy.wait_send()
        if i >= len(far):
            copy.wait_recv()
    for copy in passes:
        copy.wait()


def exchange(hidden_rows, weights, gains, kv_cache, count):
    rows, width = hidden_rows.shape
    line = count // PAIR
    total = rows * count
    tiles = total // (2 * HD)
    dma = pltpu.SemaphoreType.DMA
    whole = pl.BlockSpec(memory_space=pl.ANY)
    vmem = pl.BlockSpec(memory_space=pltpu.VMEM)
    return pl.pallas_call(
        functools.partial(exchange_kernel, count),
        out_shape=(
            jax.ShapeDtypeStruct((3, total, 3 * HD), hidden_rows.dtype),
            jax.ShapeDtypeStruct((2, kv_cache.shape[1] * count, 3 * HD), kv_cache.dtype),
        ),
        in_specs=[whole, whole, vmem, whole],
        out_specs=[vmem, whole],
        scratch_shapes=[
            pltpu.VMEM((total, width), jnp.bfloat16),
            pltpu.VMEM((6 * HD, width), jnp.bfloat16),
            pltpu.VMEM((3 * HD, width), jnp.bfloat16),
            pltpu.VMEM((2, total, 3 * HD), jnp.float32),
            pltpu.VMEM((2 * tiles, 2 * HD), jnp.float32),
            pltpu.VMEM((3, total, HD), jnp.bfloat16),
            pltpu.VMEM((3, total, HD), jnp.bfloat16),
            pltpu.VMEM((2 * count, 2 * tiles, 2 * HD), jnp.float32),
            dma((2 * count,)), dma((line,)), dma((line,)), dma((2 * line - 1,)),
            dma((2 * (2 * line - 1),)), dma((2 * count,)), dma((2 * count,)), dma((9,)),
            dma((2 * count,)), dma((2 * count,)), dma((count,)), dma((count,)), dma((2,)),
        ],
        compiler_params=pltpu.CompilerParams(
            collective_id=0, has_side_effects=True, vmem_limit_bytes=VMEM_LIMIT
        ),
    )(hidden_rows, weights, gains, kv_cache)


def attend_kernel(starts_ref, side_ref, query_ref, cache_ref, newer_ref, pair_ref, middle_ref, held):
    step = pl.program_id(0)

    @pl.when(step % 4 == 0)
    def _():
        held[...] = cache_ref[...]
        for number in range(NBLK):
            at = pl.multiple_of(starts_ref[number], BLK)
            held[:, pl.ds(at, BLK), :] = newer_ref[:, number * BLK : (number + 1) * BLK, :]

    scores = lax.dot_general(
        query_ref[...], held[0], (((1,), (1,)), ((), ())), preferred_element_type=jnp.float32
    )
    top = jnp.max(scores, axis=1, keepdims=True)
    weights = jnp.exp((scores - top) * HD ** (-0.5))
    total = jnp.sum(weights, axis=1, keepdims=True)
    summed = jnp.dot(weights.astype(jnp.bfloat16), held[1], preferred_element_type=jnp.float32)
    result = (summed / total).astype(jnp.bfloat16)

    @pl.when(step < 8)
    def _():
        pair_ref[...] = result

    @pl.when(step >= 8)
    def _():
        middle_ref[...] = result


def attend(block_starts, side, query, spread, newer):
    rows = query.shape[0]
    positions = spread.shape[1]
    tiles = rows // TILE

    def query_at(u, starts, side):
        inner = jnp.where(u < 2 * tiles, u % tiles, side[0] * (tiles // 2) + u - 2 * tiles)
        return inner, u // tiles

    def pair_at(u, starts, side):
        v = jnp.minimum(u, 2 * tiles - 1)
        return v % tiles, v // tiles

    return pl.pallas_call(
        attend_kernel,
        out_shape=(
            jax.ShapeDtypeStruct((rows, 2 * HD), jnp.bfloat16),
            jax.ShapeDtypeStruct((rows // 2, HD), jnp.bfloat16),
        ),
        grid_spec=pltpu.PrefetchScalarGridSpec(
            num_scalar_prefetch=2,
            grid=(2 * tiles + tiles // 2,),
            in_specs=[
                pl.BlockSpec((TILE, HD), query_at),
                pl.BlockSpec((2, positions, HD), lambda u, starts, side: (0, 0, u // tiles)),
                pl.BlockSpec((2, rows, HD), lambda u, starts, side: (0, 0, u // tiles)),
            ],
            out_specs=[
                pl.BlockSpec((TILE, HD), pair_at),
                pl.BlockSpec((TILE, HD), lambda u, starts, side: (jnp.maximum(u - 2 * tiles, 0), 0)),
            ],
            scratch_shapes=[pltpu.VMEM((2, positions, HD), jnp.bfloat16)],
        ),
        compiler_params=pltpu.CompilerParams(vmem_limit_bytes=VMEM_LIMIT),
    )(block_starts, side, query, spread, newer)


def collect_kernel(count, pair_ref, middle_ref, full_ref, recv_sem, up_sem, down_sem, side_sem, own_sem):
    me = lax.axis_index("seq")
    line = count // PAIR
    z, x = me // PAIR, me % PAIR
    rows = pair_ref.shape[0]
    group = full_ref.shape[1] // line
    above, below = {"seq": me + PAIR}, {"seq": me - PAIR}
    partner = {"seq": z * PAIR + 1 - x}

    barrier = pltpu.get_barrier_semaphore()

    def greet(where):
        pl.semaphore_signal(barrier, inc=1, device_id=where, device_id_type=MESH)

    @pl.when(z < line - 1)
    def _():
        greet(above)

    @pl.when(z > 0)
    def _():
        greet(below)

    greet(partner)
    neighbours = 1 + (z < line - 1).astype(jnp.int32) + (z > 0).astype(jnp.int32)
    pl.semaphore_wait(barrier, neighbours)

    def spots(owner):
        to_z, to_x = owner // PAIR, owner % PAIR
        pair_at = pl.multiple_of(to_z * group + to_x * 3 * HD, HD)
        middle_at = pl.multiple_of(to_z * group + 2 * HD, HD)
        low = pl.multiple_of(to_x * (rows // 2), rows // 2)
        return (
            full_ref.at[:, pl.ds(pair_at, 2 * HD)],
            full_ref.at[pl.ds(low, rows // 2), pl.ds(middle_at, HD)],
        )

    own_blocks = (pair_ref, middle_ref)

    def relay(owner, sem, at, where, first=False):
        return [
            remote(own_blocks[i] if first else spot, spot, sem.at[2 * at + i], recv_sem.at[2 * owner + i], where)
            for i, spot in enumerate(spots(owner))
        ]

    def start(*args):
        for copy in relay(*args):
            copy.start()

    def arrived(owner):
        for copy in relay(owner, side_sem, 0, partner):
            copy.wait_recv()

    def sent(sem, at, where):
        for copy in relay(me, sem, at, where):
            copy.wait_send()

    @pl.when(z < line - 1)
    def _():
        start(me, up_sem, 0, above, True)

    @pl.when(z > 0)
    def _():
        start(me, down_sem, 0, below, True)

    start(me, side_sem, line - 1, partner, True)
    own = [
        pltpu.make_async_copy(block, spot, own_sem.at[i])
        for i, (block, spot) in enumerate(zip(own_blocks, spots(me)))
    ]
    for copy in own:
        copy.start()

    def handle_low(d):
        @pl.when(z - d >= 0)
        def _():
            owner = me - d * PAIR
            arrived(owner)

            @pl.when(z < line - 1)
            def _():
                start(owner, up_sem, d, above)

            start(owner, side_sem, line - 1 - d, partner)

    def handle_high(d):
        @pl.when(z + d < line)
        def _():
            owner = me + d * PAIR
            arrived(owner)

            @pl.when(z > 0)
            def _():
                start(owner, down_sem, d, below)

            start(owner, side_sem, line - 1 + d, partner)

    for d in range(1, line):
        handle_low(d)
        handle_high(d)
    for copy in own:
        copy.wait()

    for d in range(1 - line, line):
        @pl.when(jnp.logical_and(z + d >= 0, z + d < line))
        def _():
            arrived((z + d) * PAIR + 1 - x)
            sent(side_sem, line - 1 + d, partner)

    for d in range(line):
        @pl.when(jnp.logical_and(z < line - 1, z - d >= 0))
        def _():
            sent(up_sem, d, above)

        @pl.when(jnp.logical_and(z > 0, z + d < line))
        def _():
            sent(down_sem, d, below)


def collect(pair, middle, count, width):
    line = count // PAIR
    dma = pltpu.SemaphoreType.DMA
    return pl.pallas_call(
        functools.partial(collect_kernel, count),
        out_shape=jax.ShapeDtypeStruct((pair.shape[0], width), pair.dtype),
        in_specs=[pl.BlockSpec(memory_space=pl.ANY)] * 2,
        out_specs=pl.BlockSpec(memory_space=pl.ANY),
        scratch_shapes=[
            dma((2 * count,)), dma((2 * line,)), dma((2 * line,)), dma((2 * (2 * line - 1),)), dma((2,)),
        ],
        compiler_params=pltpu.CompilerParams(
            collective_id=1, has_side_effects=True, vmem_limit_bytes=VMEM_LIMIT
        ),
    )(pair, middle)


def by_heads(hidden_rows, block_starts, w_qkv, qk_gain, kv_cache, w_out):
    count = lax.axis_size("seq")
    side = lax.axis_index("seq") % PAIR
    columns = w_qkv.shape[2]
    features = kv_cache.shape[2]
    weights = jnp.transpose(w_qkv, (1, 2, 0)).reshape(3 * columns, w_qkv.shape[0])
    part = columns - 2 * HD
    blank = jnp.zeros((2, part), qk_gain.dtype)
    gains = jnp.where(
        side == 0,
        jnp.concatenate([qk_gain, blank], axis=1),
        jnp.concatenate([qk_gain[:, part:], blank, qk_gain[:, :part]], axis=1),
    )
    heads, spread = exchange(hidden_rows, weights, gains, kv_cache, count)
    pair, middle = attend(
        block_starts, side.reshape(1).astype(jnp.int32), heads[0], spread, heads[1:]
    )
    gathered = collect(pair, middle, count, features)
    return lax.psum_scatter(
        jnp.dot(gathered, w_out, preferred_element_type=jnp.float32).astype(jnp.bfloat16),
        "head",
        scatter_dimension=0,
        tiled=True,
    )


def shifted(block, axis, distance):
    devices = range(lax.axis_size(axis))
    route = [((i - distance) % len(devices), i) for i in devices]
    return lax.ppermute(block, axis, route)


def write_blocks(kv_cache, newer, block_starts):
    length = kv_cache.shape[1]
    first = lax.axis_index("seq") * length
    cache = kv_cache
    for number in range(NBLK):
        offset = block_starts[number] - first
        inside = jnp.logical_and(offset >= 0, offset < length)
        place = jnp.clip(offset, 0, length - BLK)
        block = jnp.transpose(newer[number * BLK : (number + 1) * BLK], (1, 0, 2))
        present = lax.dynamic_slice_in_dim(cache, place, BLK, 1)
        cache = lax.dynamic_update_slice_in_dim(cache, jnp.where(inside, block, present), place, 1)
    return cache


def by_positions(hidden_rows, block_starts, w_qkv, qk_gain, kv_cache, w_out):
    columns = w_qkv.shape[2]
    flat_w = w_qkv.reshape(w_qkv.shape[0], 3 * columns)
    piece = lax.all_gather(hidden_rows, "seq", axis=0, tiled=True)
    projected = jnp.dot(piece, flat_w, preferred_element_type=jnp.float32).reshape(
        piece.shape[0], 3, columns
    )
    paired = projected[:, :2]
    squares = jnp.sum(paired * paired, axis=2)
    totals = lax.psum(squares, ("head", "seq"))
    factor = lax.rsqrt(totals / (HEADS * HD) + 1e-06)
    normed = paired * factor[:, :, None] * qk_gain[None]
    fresh = jnp.concatenate([normed, projected[:, 2:]], axis=1).astype(jnp.bfloat16)
    features = kv_cache.shape[2]
    heads = features // HD
    length = kv_cache.shape[1]
    own = lax.all_to_all(fresh, "seq", split_axis=0, concat_axis=2, tiled=True)
    newer = lax.all_gather(own[:, 1:], "seq", axis=0, tiled=True)
    cache = write_blocks(kv_cache, newer, block_starts)
    keys = cache[0].reshape(length, heads, HD)
    values = cache[1].reshape(length, heads, HD)
    rows = own.shape[0]
    query_rows = own[:, 0].reshape(rows, heads, HD)
    start_state = (
        query_rows,
        jnp.full((rows, heads), -1e30, jnp.float32),
        jnp.zeros((rows, heads), jnp.float32),
        jnp.zeros((rows, heads, HD), jnp.float32),
    )

    def visit(step, state):
        query_now, top_old, total_old, summed_old = state
        scores = jnp.einsum(
            "rhd,thd->hrt", query_now, keys, preferred_element_type=jnp.float32
        ) * HD ** (-0.5)
        top_new = jnp.maximum(top_old, jnp.max(scores, axis=2).T)
        weights = jnp.exp(scores - top_new.T[:, :, None])
        decay = jnp.exp(top_old - top_new)
        total_new = total_old * decay + jnp.sum(weights, axis=2).T
        summed_new = summed_old * decay[:, :, None] + jnp.einsum(
            "hrt,thd->rhd", weights.astype(jnp.bfloat16), values, preferred_element_type=jnp.float32
        )
        return (
            shifted(query_now, "seq", 1),
            shifted(top_new.astype(jnp.bfloat16), "seq", 1).astype(top_new.dtype),
            shifted(total_new.astype(jnp.bfloat16), "seq", 1).astype(total_new.dtype),
            shifted(summed_new.astype(jnp.bfloat16), "seq", 1).astype(summed_new.dtype),
        )

    final = lax.fori_loop(0, lax.axis_size("seq"), visit, start_state)
    summed = final[3]
    total = final[2]
    attended = (summed / total[:, :, None]).astype(jnp.bfloat16).reshape(summed.shape[0], features)
    gathered = lax.all_gather(attended, "seq", axis=0, tiled=True)
    result = lax.psum_scatter(
        jnp.dot(gathered, w_out, preferred_element_type=jnp.float32).astype(jnp.bfloat16),
        "head",
        scatter_dimension=0,
        tiled=True,
    )
    return result


def solution(mesh):
    count = mesh.shape["seq"]
    split = mesh.shape["head"] * count
    fits = mesh.shape["head"] == 2 and count % PAIR == 0 and HEADS * PAIR == 5 * split
    return jax.shard_map(
        by_heads if fits else by_positions,
        mesh=mesh,
        in_specs=(
            P(("grp", "seq"), None),
            P("grp"),
            P(None, None, ("head", "seq")),
            P(None, ("head", "seq")),
            P(None, ("grp", "seq"), "head"),
            P("head", "seq"),
        ),
        out_specs=P(("grp", "head"), "seq"),
        check_vma=False,
    )
```

```python
import functools

import jax
import jax.numpy as jnp
from jax import lax
from jax.experimental import pallas as pl
from jax.experimental.pallas import tpu as pltpu
from jax.sharding import PartitionSpec as P

HEADS = 40
HD = 128
BLK = 128
NBLK = 8
PAIR = 2
TILE = 256
MESH = pl.DeviceIdType.MESH
VMEM_LIMIT = 56 * 1024 * 1024


def remote(src, dst, send, recv, where):
    return pltpu.make_async_remote_copy(
        src_ref=src, dst_ref=dst, send_sem=send, recv_sem=recv, device_id=where, device_id_type=MESH
    )


def exchange_kernel(
    count, hidden_ref, weight_ref, gain_ref, cache_ref, fresh_ref, spread_ref,
    full, pair_w, middle_w, projected, shared, mine_mid, theirs_mid, sums,
    recv_sem, up_sem, down_sem, side_sem, core_sem, kv_send, kv_recv, own_sem,
    sum_send, sum_recv, pass_send, pass_recv, mid_sem,
):
    me = lax.axis_index("seq")
    core = lax.axis_index("head")
    line = count // PAIR
    z, x = me // PAIR, me % PAIR
    rows = hidden_ref.shape[0]
    half = rows // 2
    length = cache_ref.shape[1]
    group = cache_ref.shape[2] // line
    columns = weight_ref.shape[0] // 3
    own_part = columns - 2 * HD
    above, below = {"seq": me + PAIR}, {"seq": me - PAIR}
    partner_at = z * PAIR + 1 - x
    partner = {"seq": partner_at}
    other = {"head": 1 - core}
    peers = [
        (lax.rem(core + c, 2), lax.rem(me + step, count))
        for c in range(2)
        for step in range(count)
        if c or step
    ]

    barrier = pltpu.get_barrier_semaphore()
    for to_core, to in peers:
        pl.semaphore_signal(barrier, inc=1, device_id={"head": to_core, "seq": to}, device_id_type=MESH)
    pl.semaphore_wait(barrier, 2 * count - 1)

    def place(owner, part):
        return full.at[pl.ds(pl.multiple_of(owner * rows + part * half, half), half), :]

    mine = hidden_ref.at[pl.ds(pl.multiple_of(core * half, half), half), :]

    def relay(owner, part, sem, where, src=None):
        spot = place(owner, part)
        return remote(spot if src is None else src, spot, sem, recv_sem.at[owner * 2 + part], where)

    @pl.when(z < line - 1)
    def _():
        relay(me, core, up_sem.at[0], above, mine).start()

    @pl.when(z > 0)
    def _():
        relay(me, core, down_sem.at[0], below, mine).start()

    relay(me, core, side_sem.at[line - 1], partner, mine).start()
    loads = [
        pltpu.make_async_copy(
            hidden_ref, full.at[pl.ds(pl.multiple_of(me * rows, rows), rows), :], own_sem.at[0]
        )
    ]
    for c in range(3):
        pair_at = pl.multiple_of(c * columns + x * own_part, 16)
        middle_at = pl.multiple_of(c * columns + (1 - x) * 2 * HD, 16)
        into = pl.multiple_of(c * HD + x * own_part, 16)
        away = pl.multiple_of(c * HD + (1 - x) * own_part, 16)
        loads.append(
            pltpu.make_async_copy(
                weight_ref.at[pl.ds(pair_at, 2 * HD), :], pair_w.at[pl.ds(c * 2 * HD, 2 * HD), :], own_sem.at[1 + c]
            )
        )
        loads.append(
            pltpu.make_async_copy(
                weight_ref.at[pl.ds(middle_at, own_part), :], middle_w.at[pl.ds(into, own_part), :], own_sem.at[4 + c]
            )
        )
        middle_w[pl.ds(away, own_part), :] = jnp.zeros((own_part, middle_w.shape[1]), middle_w.dtype)
    for copy in loads:
        copy.start()

    def arrived(owner, part):
        relay(owner, part, core_sem.at[0], other).wait_recv()

    def handle_low(d):
        @pl.when(z - d >= 0)
        def _():
            owner = me - d * PAIR
            arrived(owner, core)

            @pl.when(z < line - 1)
            def _():
                relay(owner, core, up_sem.at[d], above).start()

            relay(owner, core, side_sem.at[line - 1 - d], partner).start()
            relay(owner, core, core_sem.at[line - 1 - d], other).start()

    def handle_high(d):
        @pl.when(z + d < line)
        def _():
            owner = me + d * PAIR
            arrived(owner, core)

            @pl.when(z > 0)
            def _():
                relay(owner, core, down_sem.at[d], below).start()

            relay(owner, core, side_sem.at[line - 1 + d], partner).start()
            relay(owner, core, core_sem.at[line - 1 + d], other).start()

    def handle_side(d):
        @pl.when(jnp.logical_and(z + d >= 0, z + d < line))
        def _():
            owner = (z + d) * PAIR + 1 - x
            arrived(owner, core)
            relay(owner, core, core_sem.at[2 * line - 1 + line - 1 + d], other).start()

    def source(owner):
        return owner // PAIR, owner % PAIR

    def pair_copy(step, to):
        to_z, to_x = source(to)
        at = pl.multiple_of(to_z * group + to_x * 3 * HD, HD)
        src = cache_ref.at[:, :, pl.ds(at, 2 * HD)]
        dst = spread_ref.at[:, pl.ds(pl.multiple_of(me * length, length), length), pl.ds(0, 2 * HD)]
        return src, dst

    part = length // 2

    def middle_slot(owner, which):
        at = pl.multiple_of(owner * length + which * part, part)
        return spread_ref.at[:, pl.ds(at, part), pl.ds(2 * HD, HD)]

    def middle_copy(to):
        to_z, to_x = source(to)
        at = pl.multiple_of(to_z * group + 2 * HD, HD)
        low = pl.multiple_of(to_x * part, part)
        return cache_ref.at[:, pl.ds(low, part), pl.ds(at, HD)], middle_slot(me, to_x)

    middle_at = pl.multiple_of(z * group + 2 * HD, HD)
    whole_middle = (
        cache_ref.at[:, :, pl.ds(middle_at, HD)],
        spread_ref.at[:, pl.ds(pl.multiple_of(me * length, length), length), pl.ds(2 * HD, HD)],
    )
    locals_ = [
        pltpu.make_async_copy(*pair_copy(0, me), own_sem.at[7]),
        pltpu.make_async_copy(*whole_middle, own_sem.at[8]),
    ]
    far = []
    for hop in range(1, line):
        for across in range(PAIR):
            to = lax.rem(z + hop, line) * PAIR + lax.rem(x + across, PAIR)
            far.append((hop * PAIR + across, to, lax.rem(z + line - hop, line) * PAIR + lax.rem(x + across, PAIR)))
    sends = []
    for slot, to, _ in far:
        sends.append(remote(*middle_copy(to), kv_send.at[2 * slot], kv_recv.at[2 * slot], {"seq": to}))
    sends.append(remote(*whole_middle, kv_send.at[0], kv_recv.at[0], partner))
    for slot, to, _ in far:
        sends.append(remote(*pair_copy(slot, to), kv_send.at[2 * slot + 1], kv_recv.at[2 * slot + 1], {"seq": to}))
    sends.append(remote(*pair_copy(0, partner_at), kv_send.at[1], kv_recv.at[1], partner))

    for d in range(line):
        if d + 1 < line:
            handle_low(d + 1)
            handle_high(d + 1)
        if d + 1 == max(line - 2, 1):
            for copy in sends + locals_:
                copy.start()
        handle_side(d)
        if d:
            handle_side(-d)

    for copy in loads:
        copy.wait()
    for step in range(1, count):
        arrived(lax.rem(me + step, count), 1 - core)

    tile = 2 * HD
    tiles = full.shape[0] // tile
    nt = (((1,), (1,)), ((), ()))

    @pl.loop(0, tiles)
    def _(t):
        at = pl.ds(pl.multiple_of(t * tile, tile), tile)
        lines = full[at, :]
        for c in range(3):
            wide = lax.dot_general(
                lines, pair_w[c * 2 * HD : (c + 1) * 2 * HD, :], nt, preferred_element_type=jnp.float32
            )
            thin = lax.dot_general(
                lines, middle_w[c * HD : (c + 1) * HD, :], nt, preferred_element_type=jnp.float32
            )
            if c == 2:
                fresh_ref[2, at, 0 : 2 * HD] = wide.astype(jnp.bfloat16)
                mine_mid[2, at, :] = thin.astype(jnp.bfloat16)
            else:
                projected[c, at, 0 : 2 * HD] = wide
                projected[c, at, 2 * HD : 3 * HD] = thin
                square = jnp.sum(wide * wide, axis=1, keepdims=True) + jnp.sum(thin * thin, axis=1, keepdims=True)
                turned = jnp.transpose(jnp.broadcast_to(square, (tile, HD)))
                sums[0, pl.ds(c * tiles + t, 1), :] = turned[0:1, :]

    shares = []
    for i, (to_core, to) in enumerate(peers):
        shares.append(
            remote(
                sums.at[0], sums.at[i + 1], sum_send.at[i], sum_recv.at[i], {"head": to_core, "seq": to}
            )
        )
    for copy in shares:
        copy.start()
    for copy in shares:
        copy.wait()
    total = sums[0]
    for i in range(1, 2 * count):
        total = total + sums[i]
    shared[...] = lax.rsqrt(total / (HEADS * HD) + 1e-06)

    @pl.loop(0, tiles)
    def _(t):
        at = pl.ds(pl.multiple_of(t * tile, tile), tile)
        for c in range(2):
            factor = jnp.transpose(jnp.broadcast_to(shared[pl.ds(c * tiles + t, 1), :], (HD, tile)))
            for k in range(3):
                lanes = slice(k * HD, (k + 1) * HD)
                normed = (projected[c, at, lanes] * factor * gain_ref[c : c + 1, lanes]).astype(jnp.bfloat16)
                if k < 2:
                    fresh_ref[c, at, lanes] = normed
                else:
                    mine_mid[c, at, :] = normed

    swap = remote(mine_mid, theirs_mid, mid_sem.at[0], mid_sem.at[1], partner)
    swap.start()

    passes = []
    for slot, to, owner in far:
        remote(*middle_copy(to), kv_send.at[2 * slot], kv_recv.at[2 * slot], {"seq": to}).wait_recv()
        spot = middle_slot(owner, x)
        copy = remote(spot, spot, pass_send.at[slot], pass_recv.at[slot], partner)
        copy.start()
        passes.append(copy)

    swap.wait()

    @pl.loop(0, tiles)
    def _(t):
        at = pl.ds(pl.multiple_of(t * tile, tile), tile)
        for c in range(3):
            fresh_ref[c, at, 2 * HD : 3 * HD] = mine_mid[c, at, :] + theirs_mid[c, at, :]

    def sent(owner, sem, where):
        relay(owner, core, sem, where).wait_send()

    for d in range(line):
        @pl.when(jnp.logical_and(z < line - 1, z - d >= 0))
        def _():
            sent(me, up_sem.at[d], above)

        @pl.when(jnp.logical_and(z > 0, z + d < line))
        def _():
            sent(me, down_sem.at[d], below)

    for d in range(1 - line, line):
        @pl.when(jnp.logical_and(z + d >= 0, z + d < line))
        def _():
            sent(me, side_sem.at[line - 1 + d], partner)
            if d:
                sent(me, core_sem.at[line - 1 + d], other)
            sent(me, core_sem.at[2 * line - 1 + line - 1 + d], other)

    for copy in locals_:
        copy.wait()
    for i, copy in enumerate(sends):
        copy.wait_send()
        if i >= len(far):
            copy.wait_recv()
    for copy in passes:
        copy.wait()


def exchange(hidden_rows, weights, gains, kv_cache, count):
    rows, width = hidden_rows.shape
    line = count // PAIR
    total = rows * count
    tiles = total // (2 * HD)
    dma = pltpu.SemaphoreType.DMA
    whole = pl.BlockSpec(memory_space=pl.ANY)
    vmem = pl.BlockSpec(memory_space=pltpu.VMEM)
    return pl.pallas_call(
        functools.partial(exchange_kernel, count),
        out_shape=(
            jax.ShapeDtypeStruct((3, total, 3 * HD), hidden_rows.dtype),
            jax.ShapeDtypeStruct((2, kv_cache.shape[1] * count, 3 * HD), kv_cache.dtype),
        ),
        in_specs=[whole, whole, vmem, whole],
        out_specs=[vmem, whole],
        scratch_shapes=[
            pltpu.VMEM((total, width), jnp.bfloat16),
            pltpu.VMEM((6 * HD, width), jnp.bfloat16),
            pltpu.VMEM((3 * HD, width), jnp.bfloat16),
            pltpu.VMEM((2, total, 3 * HD), jnp.float32),
            pltpu.VMEM((2 * tiles, 2 * HD), jnp.float32),
            pltpu.VMEM((3, total, HD), jnp.bfloat16),
            pltpu.VMEM((3, total, HD), jnp.bfloat16),
            pltpu.VMEM((2 * count, 2 * tiles, 2 * HD), jnp.float32),
            dma((2 * count,)), dma((line,)), dma((line,)), dma((2 * line - 1,)),
            dma((2 * (2 * line - 1),)), dma((2 * count,)), dma((2 * count,)), dma((9,)),
            dma((2 * count,)), dma((2 * count,)), dma((count,)), dma((count,)), dma((2,)),
        ],
        compiler_params=pltpu.CompilerParams(
            collective_id=0, has_side_effects=True, vmem_limit_bytes=VMEM_LIMIT
        ),
    )(hidden_rows, weights, gains, kv_cache)


def write_kernel(starts_ref, heads_ref, spread_ref, out_ref, sems):
    copies = [
        pltpu.make_async_copy(
            heads_ref.at[pl.ds(1, 2), pl.ds(number * BLK, BLK), :],
            out_ref.at[:, pl.ds(pl.multiple_of(starts_ref[number], BLK), BLK), :],
            sems.at[number],
        )
        for number in range(NBLK)
    ]
    for copy in copies:
        copy.start()
    for copy in copies:
        copy.wait()


def write_rows(block_starts, heads, spread):
    whole = pl.BlockSpec(memory_space=pl.ANY)
    return pl.pallas_call(
        write_kernel,
        out_shape=jax.ShapeDtypeStruct(spread.shape, spread.dtype),
        in_specs=[pl.BlockSpec(memory_space=pltpu.SMEM), whole, whole],
        out_specs=whole,
        scratch_shapes=[pltpu.SemaphoreType.DMA((NBLK,))],
        input_output_aliases={2: 0},
        compiler_params=pltpu.CompilerParams(vmem_limit_bytes=VMEM_LIMIT),
    )(block_starts, heads, spread)


UNITS = 5


def finish_kernel(
    count, heads_ref, spread_ref, w_ref, out_ref,
    query, cache, weight, full, total, give, got,
    load_sem, recv_sem, up_sem, down_sem, side_sem, core_sem,
):
    me = lax.axis_index("seq")
    core = lax.axis_index("head")
    line = count // PAIR
    z, x = me // PAIR, me % PAIR
    rows = full.shape[0]
    low = rows // 2
    group = full.shape[1] // line
    above, below = {"seq": me + PAIR}, {"seq": me - PAIR}
    partner = {"seq": z * PAIR + 1 - x}
    other = {"head": 1 - core}

    loads = [pltpu.make_async_copy(heads_ref.at[0], query, load_sem.at[0])]
    for head in range(3):
        lanes = pl.ds(head * HD, HD)
        loads.append(pltpu.make_async_copy(spread_ref.at[:, :, lanes], cache.at[:, :, lanes], load_sem.at[1 + head]))
    loads.append(pltpu.make_async_copy(w_ref, weight, load_sem.at[4]))
    for copy in loads:
        copy.start()

    barrier = pltpu.get_barrier_semaphore()

    def greet(where):
        pl.semaphore_signal(barrier, inc=1, device_id=where, device_id_type=MESH)

    @pl.when(z < line - 1)
    def _():
        greet(above)

    @pl.when(z > 0)
    def _():
        greet(below)

    greet(partner)
    greet(other)
    neighbours = 2 + (z < line - 1).astype(jnp.int32) + (z > 0).astype(jnp.int32)
    pl.semaphore_wait(barrier, neighbours)

    def corner(owner, unit):
        to_z, to_x = owner // PAIR, owner % PAIR
        if unit == UNITS - 1:
            return to_x * low, to_z * group + 2 * HD
        return (unit % 2) * low, to_z * group + to_x * 3 * HD + (unit // 2) * HD

    def spot(owner, unit):
        down, along = corner(owner, unit)
        return full.at[pl.ds(pl.multiple_of(down, low), low), pl.ds(pl.multiple_of(along, HD), HD)]

    def relay(owner, unit, sem, at, where):
        place = spot(owner, unit)
        return remote(place, place, sem.at[UNITS * at + unit], recv_sem.at[UNITS * owner + unit], where)

    def arrived(owner, unit):
        relay(owner, unit, side_sem, 0, partner).wait_recv()

    def attend(unit):
        head = unit // 2
        if unit % 2 == 0:
            loads[1 + head].wait()
        down, along = corner(me, unit)
        lanes = slice(head * HD, (head + 1) * HD)

        @pl.loop(0, low // TILE)
        def _(t):
            at = pl.ds(pl.multiple_of(down + t * TILE, TILE), TILE)
            scores = lax.dot_general(
                query[at, lanes], cache[0, :, lanes], (((1,), (1,)), ((), ())), preferred_element_type=jnp.float32
            )
            top = jnp.max(scores, axis=1, keepdims=True)
            weights = jnp.exp((scores - top) * HD ** (-0.5))
            mass = jnp.sum(weights, axis=1, keepdims=True)
            summed = jnp.dot(weights.astype(jnp.bfloat16), cache[1, :, lanes], preferred_element_type=jnp.float32)
            full[at, pl.ds(pl.multiple_of(along, HD), HD)] = (summed / mass).astype(jnp.bfloat16)

    def send_own(unit):
        @pl.when(z < line - 1)
        def _():
            relay(me, unit, up_sem, 0, above).start()

        @pl.when(z > 0)
        def _():
            relay(me, unit, down_sem, 0, below).start()

        relay(me, unit, side_sem, line - 1, partner).start()

    def handle(unit, d):
        @pl.when(z - d >= 0)
        def _():
            owner = me - d * PAIR
            arrived(owner, unit)

            @pl.when(z < line - 1)
            def _():
                relay(owner, unit, up_sem, d, above).start()

            relay(owner, unit, side_sem, line - 1 - d, partner).start()

        @pl.when(z + d < line)
        def _():
            owner = me + d * PAIR
            arrived(owner, unit)

            @pl.when(z > 0)
            def _():
                relay(owner, unit, down_sem, d, below).start()

            relay(owner, unit, side_sem, line - 1 + d, partner).start()

    def multiply(d):
        @pl.when(jnp.logical_and(z + d >= 0, z + d < line))
        def _():
            for unit in range(UNITS):
                arrived((z + d) * PAIR + 1 - x, unit)
            along = pl.ds(pl.multiple_of((z + d) * group, group), group)

            @pl.loop(0, rows // TILE)
            def _(t):
                at = pl.ds(pl.multiple_of(t * TILE, TILE), TILE)
                part = jnp.dot(full[at, along], weight[along, :], preferred_element_type=jnp.float32)
                if d == 0:
                    total[at, :] = part
                else:
                    total[at, :] = total[at, :] + part

    loads[0].wait()
    for stage in range(UNITS + line - 1):
        if stage < UNITS:
            attend(stage)
            send_own(stage)
        for d in range(1, line):
            if 0 <= stage - d < UNITS:
                handle(stage - d, d)
        d = stage - UNITS
        if d == 0:
            loads[4].wait()
            multiply(0)
        elif d > 0:
            multiply(-d)
            multiply(d)
    multiply(1 - line)
    multiply(line - 1)

    theirs = pl.ds(pl.multiple_of((1 - core) * low, low), low)
    ours = pl.ds(pl.multiple_of(core * low, low), low)
    give[...] = total[theirs, :].astype(jnp.bfloat16)
    swap = remote(give, got, core_sem.at[0], core_sem.at[1], other)
    swap.start()

    for unit in range(UNITS):
        for d in range(line):
            @pl.when(jnp.logical_and(z < line - 1, z - d >= 0))
            def _():
                relay(me, unit, up_sem, d, above).wait_send()

            @pl.when(jnp.logical_and(z > 0, z + d < line))
            def _():
                relay(me, unit, down_sem, d, below).wait_send()

        for d in range(1 - line, line):
            @pl.when(jnp.logical_and(z + d >= 0, z + d < line))
            def _():
                relay(me, unit, side_sem, line - 1 + d, partner).wait_send()

    swap.wait()
    out_ref[...] = (total[ours, :] + got[...].astype(jnp.float32)).astype(jnp.bfloat16)


def finish(heads, spread, w_out, count):
    rows = heads.shape[1]
    features, width = w_out.shape
    line = count // PAIR
    dma = pltpu.SemaphoreType.DMA
    whole = pl.BlockSpec(memory_space=pl.ANY)
    return pl.pallas_call(
        functools.partial(finish_kernel, count),
        out_shape=jax.ShapeDtypeStruct((rows // 2, width), w_out.dtype),
        in_specs=[whole] * 3,
        out_specs=pl.BlockSpec(memory_space=pltpu.VMEM),
        scratch_shapes=[
            pltpu.VMEM(heads.shape[1:], jnp.bfloat16),
            pltpu.VMEM(spread.shape, jnp.bfloat16),
            pltpu.VMEM(w_out.shape, jnp.bfloat16),
            pltpu.VMEM((rows, features), jnp.bfloat16),
            pltpu.VMEM((rows, width), jnp.float32),
            pltpu.VMEM((rows // 2, width), jnp.bfloat16),
            pltpu.VMEM((rows // 2, width), jnp.bfloat16),
            dma((5,)), dma((UNITS * count,)), dma((UNITS * line,)), dma((UNITS * line,)),
            dma((UNITS * (2 * line - 1),)), dma((2,)),
        ],
        compiler_params=pltpu.CompilerParams(
            collective_id=1, has_side_effects=True, vmem_limit_bytes=VMEM_LIMIT
        ),
    )(heads, spread, w_out)


def by_heads(hidden_rows, block_starts, w_qkv, qk_gain, kv_cache, w_out):
    count = lax.axis_size("seq")
    side = lax.axis_index("seq") % PAIR
    columns = w_qkv.shape[2]
    weights = jnp.transpose(w_qkv, (1, 2, 0)).reshape(3 * columns, w_qkv.shape[0])
    part = columns - 2 * HD
    blank = jnp.zeros((2, part), qk_gain.dtype)
    gains = jnp.where(
        side == 0,
        jnp.concatenate([qk_gain, blank], axis=1),
        jnp.concatenate([qk_gain[:, part:], blank, qk_gain[:, :part]], axis=1),
    )
    heads, spread = exchange(hidden_rows, weights, gains, kv_cache, count)
    spread = write_rows(block_starts, heads, spread)
    return finish(heads, spread, w_out, count)


def shifted(block, axis, distance):
    devices = range(lax.axis_size(axis))
    route = [((i - distance) % len(devices), i) for i in devices]
    return lax.ppermute(block, axis, route)


def write_blocks(kv_cache, newer, block_starts):
    length = kv_cache.shape[1]
    first = lax.axis_index("seq") * length
    cache = kv_cache
    for number in range(NBLK):
        offset = block_starts[number] - first
        inside = jnp.logical_and(offset >= 0, offset < length)
        place = jnp.clip(offset, 0, length - BLK)
        block = jnp.transpose(newer[number * BLK : (number + 1) * BLK], (1, 0, 2))
        present = lax.dynamic_slice_in_dim(cache, place, BLK, 1)
        cache = lax.dynamic_update_slice_in_dim(cache, jnp.where(inside, block, present), place, 1)
    return cache


def by_positions(hidden_rows, block_starts, w_qkv, qk_gain, kv_cache, w_out):
    columns = w_qkv.shape[2]
    flat_w = w_qkv.reshape(w_qkv.shape[0], 3 * columns)
    piece = lax.all_gather(hidden_rows, "seq", axis=0, tiled=True)
    projected = jnp.dot(piece, flat_w, preferred_element_type=jnp.float32).reshape(
        piece.shape[0], 3, columns
    )
    paired = projected[:, :2]
    squares = jnp.sum(paired * paired, axis=2)
    totals = lax.psum(squares, ("head", "seq"))
    factor = lax.rsqrt(totals / (HEADS * HD) + 1e-06)
    normed = paired * factor[:, :, None] * qk_gain[None]
    fresh = jnp.concatenate([normed, projected[:, 2:]], axis=1).astype(jnp.bfloat16)
    features = kv_cache.shape[2]
    heads = features // HD
    length = kv_cache.shape[1]
    own = lax.all_to_all(fresh, "seq", split_axis=0, concat_axis=2, tiled=True)
    newer = lax.all_gather(own[:, 1:], "seq", axis=0, tiled=True)
    cache = write_blocks(kv_cache, newer, block_starts)
    keys = cache[0].reshape(length, heads, HD)
    values = cache[1].reshape(length, heads, HD)
    rows = own.shape[0]
    query_rows = own[:, 0].reshape(rows, heads, HD)
    start_state = (
        query_rows,
        jnp.full((rows, heads), -1e30, jnp.float32),
        jnp.zeros((rows, heads), jnp.float32),
        jnp.zeros((rows, heads, HD), jnp.float32),
    )

    def visit(step, state):
        query_now, top_old, total_old, summed_old = state
        scores = jnp.einsum(
            "rhd,thd->hrt", query_now, keys, preferred_element_type=jnp.float32
        ) * HD ** (-0.5)
        top_new = jnp.maximum(top_old, jnp.max(scores, axis=2).T)
        weights = jnp.exp(scores - top_new.T[:, :, None])
        decay = jnp.exp(top_old - top_new)
        total_new = total_old * decay + jnp.sum(weights, axis=2).T
        summed_new = summed_old * decay[:, :, None] + jnp.einsum(
            "hrt,thd->rhd", weights.astype(jnp.bfloat16), values, preferred_element_type=jnp.float32
        )
        return (
            shifted(query_now, "seq", 1),
            shifted(top_new.astype(jnp.bfloat16), "seq", 1).astype(top_new.dtype),
            shifted(total_new.astype(jnp.bfloat16), "seq", 1).astype(total_new.dtype),
            shifted(summed_new.astype(jnp.bfloat16), "seq", 1).astype(summed_new.dtype),
        )

    final = lax.fori_loop(0, lax.axis_size("seq"), visit, start_state)
    summed = final[3]
    total = final[2]
    attended = (summed / total[:, :, None]).astype(jnp.bfloat16).reshape(summed.shape[0], features)
    gathered = lax.all_gather(attended, "seq", axis=0, tiled=True)
    result = lax.psum_scatter(
        jnp.dot(gathered, w_out, preferred_element_type=jnp.float32).astype(jnp.bfloat16),
        "head",
        scatter_dimension=0,
        tiled=True,
    )
    return result


def solution(mesh):
    count = mesh.shape["seq"]
    split = mesh.shape["head"] * count
    fits = mesh.shape["head"] == 2 and count % PAIR == 0 and HEADS * PAIR == 5 * split
    return jax.shard_map(
        by_heads if fits else by_positions,
        mesh=mesh,
        in_specs=(
            P(("grp", "seq"), None),
            P("grp"),
            P(None, None, ("head", "seq")),
            P(None, ("head", "seq")),
            P(None, ("grp", "seq"), "head"),
            P("head", "seq"),
        ),
        out_specs=P(("grp", "head"), "seq"),
        check_vma=False,
    )
```

```python
import functools

import jax
import jax.numpy as jnp
from jax import lax
from jax.experimental import pallas as pl
from jax.experimental.pallas import tpu as pltpu
from jax.sharding import PartitionSpec as P

HEADS = 40
HD = 128
BLK = 128
NBLK = 8
PAIR = 2
TILE = 256
MESH = pl.DeviceIdType.MESH
VMEM_LIMIT = 56 * 1024 * 1024


def remote(src, dst, send, recv, where):
    return pltpu.make_async_remote_copy(
        src_ref=src, dst_ref=dst, send_sem=send, recv_sem=recv, device_id=where, device_id_type=MESH
    )


def exchange_kernel(
    count, hidden_ref, weight_ref, gain_ref, kv_ref, fresh_ref, spread_ref,
    cache_ref, full, pair_w, middle_w, projected, shared, mine_mid, theirs_mid, sums,
    recv_sem, up_sem, down_sem, side_sem, core_sem, kv_send, kv_recv, own_sem,
    sum_send, sum_recv, pass_send, pass_recv, mid_sem,
):
    me = lax.axis_index("seq")
    core = lax.axis_index("head")
    line = count // PAIR
    z, x = me // PAIR, me % PAIR
    rows = hidden_ref.shape[0]
    half = rows // 2
    length = cache_ref.shape[1]
    group = cache_ref.shape[2] // line
    columns = weight_ref.shape[0] // 3
    own_part = columns - 2 * HD
    above, below = {"seq": me + PAIR}, {"seq": me - PAIR}
    partner_at = z * PAIR + 1 - x
    partner = {"seq": partner_at}
    other = {"head": 1 - core}
    peers = [
        (lax.rem(core + c, 2), lax.rem(me + step, count))
        for c in range(2)
        for step in range(count)
        if c or step
    ]

    barrier = pltpu.get_barrier_semaphore()
    for to_core, to in peers:
        pl.semaphore_signal(barrier, inc=1, device_id={"head": to_core, "seq": to}, device_id_type=MESH)
    pl.semaphore_wait(barrier, 2 * count - 1)

    def place(owner, part):
        return full.at[pl.ds(pl.multiple_of(owner * rows + part * half, half), half), :]

    mine = hidden_ref.at[pl.ds(pl.multiple_of(core * half, half), half), :]

    def relay(owner, part, sem, where, src=None):
        spot = place(owner, part)
        return remote(spot if src is None else src, spot, sem, recv_sem.at[owner * 2 + part], where)

    @pl.when(z < line - 1)
    def _():
        relay(me, core, up_sem.at[0], above, mine).start()

    @pl.when(z > 0)
    def _():
        relay(me, core, down_sem.at[0], below, mine).start()

    relay(me, core, side_sem.at[line - 1], partner, mine).start()
    loads = [
        pltpu.make_async_copy(
            hidden_ref, full.at[pl.ds(pl.multiple_of(me * rows, rows), rows), :], own_sem.at[0]
        )
    ]
    for c in range(3):
        pair_at = pl.multiple_of(c * columns + x * own_part, 16)
        middle_at = pl.multiple_of(c * columns + (1 - x) * 2 * HD, 16)
        into = pl.multiple_of(c * HD + x * own_part, 16)
        away = pl.multiple_of(c * HD + (1 - x) * own_part, 16)
        loads.append(
            pltpu.make_async_copy(
                weight_ref.at[pl.ds(pair_at, 2 * HD), :], pair_w.at[pl.ds(c * 2 * HD, 2 * HD), :], own_sem.at[1 + c]
            )
        )
        loads.append(
            pltpu.make_async_copy(
                weight_ref.at[pl.ds(middle_at, own_part), :], middle_w.at[pl.ds(into, own_part), :], own_sem.at[4 + c]
            )
        )
        middle_w[pl.ds(away, own_part), :] = jnp.zeros((own_part, middle_w.shape[1]), middle_w.dtype)
    stage = pltpu.make_async_copy(kv_ref, cache_ref, own_sem.at[9])
    stage.start()
    for copy in loads:
        copy.start()

    def arrived(owner, part):
        relay(owner, part, core_sem.at[0], other).wait_recv()

    def handle_low(d):
        @pl.when(z - d >= 0)
        def _():
            owner = me - d * PAIR
            arrived(owner, core)

            @pl.when(z < line - 1)
            def _():
                relay(owner, core, up_sem.at[d], above).start()

            relay(owner, core, side_sem.at[line - 1 - d], partner).start()
            relay(owner, core, core_sem.at[line - 1 - d], other).start()

    def handle_high(d):
        @pl.when(z + d < line)
        def _():
            owner = me + d * PAIR
            arrived(owner, core)

            @pl.when(z > 0)
            def _():
                relay(owner, core, down_sem.at[d], below).start()

            relay(owner, core, side_sem.at[line - 1 + d], partner).start()
            relay(owner, core, core_sem.at[line - 1 + d], other).start()

    def handle_side(d):
        @pl.when(jnp.logical_and(z + d >= 0, z + d < line))
        def _():
            owner = (z + d) * PAIR + 1 - x
            arrived(owner, core)
            relay(owner, core, core_sem.at[2 * line - 1 + line - 1 + d], other).start()

    def source(owner):
        return owner // PAIR, owner % PAIR

    def pair_copy(step, to):
        to_z, to_x = source(to)
        at = pl.multiple_of(to_z * group + to_x * 3 * HD, HD)
        src = cache_ref.at[:, :, pl.ds(at, 2 * HD)]
        dst = spread_ref.at[:, pl.ds(pl.multiple_of(me * length, length), length), pl.ds(0, 2 * HD)]
        return src, dst

    part = length // 2

    def middle_slot(owner, which):
        at = pl.multiple_of(owner * length + which * part, part)
        return spread_ref.at[:, pl.ds(at, part), pl.ds(2 * HD, HD)]

    def middle_copy(to):
        to_z, to_x = source(to)
        at = pl.multiple_of(to_z * group + 2 * HD, HD)
        low = pl.multiple_of(to_x * part, part)
        return cache_ref.at[:, pl.ds(low, part), pl.ds(at, HD)], middle_slot(me, to_x)

    middle_at = pl.multiple_of(z * group + 2 * HD, HD)
    whole_middle = (
        cache_ref.at[:, :, pl.ds(middle_at, HD)],
        spread_ref.at[:, pl.ds(pl.multiple_of(me * length, length), length), pl.ds(2 * HD, HD)],
    )
    locals_ = [
        pltpu.make_async_copy(*pair_copy(0, me), own_sem.at[7]),
        pltpu.make_async_copy(*whole_middle, own_sem.at[8]),
    ]
    far = []
    for hop in range(1, line):
        for across in range(PAIR):
            to = lax.rem(z + hop, line) * PAIR + lax.rem(x + across, PAIR)
            far.append((hop * PAIR + across, to, lax.rem(z + line - hop, line) * PAIR + lax.rem(x + across, PAIR)))
    sends = []
    for slot, to, _ in far:
        sends.append(remote(*middle_copy(to), kv_send.at[2 * slot], kv_recv.at[2 * slot], {"seq": to}))
    sends.append(remote(*whole_middle, kv_send.at[0], kv_recv.at[0], partner))
    for slot, to, _ in far:
        sends.append(remote(*pair_copy(slot, to), kv_send.at[2 * slot + 1], kv_recv.at[2 * slot + 1], {"seq": to}))
    sends.append(remote(*pair_copy(0, partner_at), kv_send.at[1], kv_recv.at[1], partner))

    for d in range(line):
        if d + 1 < line:
            handle_low(d + 1)
            handle_high(d + 1)
        if d + 1 == max(line - 2, 1):
            stage.wait()
            for copy in sends + locals_:
                copy.start()
        handle_side(d)
        if d:
            handle_side(-d)

    for copy in loads:
        copy.wait()
    for step in range(1, count):
        arrived(lax.rem(me + step, count), 1 - core)

    tile = 2 * HD
    tiles = full.shape[0] // tile
    nt = (((1,), (1,)), ((), ()))

    @pl.loop(0, tiles)
    def _(t):
        at = pl.ds(pl.multiple_of(t * tile, tile), tile)
        lines = full[at, :]
        for c in range(3):
            wide = lax.dot_general(
                lines, pair_w[c * 2 * HD : (c + 1) * 2 * HD, :], nt, preferred_element_type=jnp.float32
            )
            thin = lax.dot_general(
                lines, middle_w[c * HD : (c + 1) * HD, :], nt, preferred_element_type=jnp.float32
            )
            if c == 2:
                fresh_ref[2, at, 0 : 2 * HD] = wide.astype(jnp.bfloat16)
                mine_mid[2, at, :] = thin.astype(jnp.bfloat16)
            else:
                projected[c, at, 0 : 2 * HD] = wide
                projected[c, at, 2 * HD : 3 * HD] = thin
                square = jnp.sum(wide * wide, axis=1, keepdims=True) + jnp.sum(thin * thin, axis=1, keepdims=True)
                turned = jnp.transpose(jnp.broadcast_to(square, (tile, HD)))
                sums[0, pl.ds(c * tiles + t, 1), :] = turned[0:1, :]

    shares = []
    for i, (to_core, to) in enumerate(peers):
        shares.append(
            remote(
                sums.at[0], sums.at[i + 1], sum_send.at[i], sum_recv.at[i], {"head": to_core, "seq": to}
            )
        )
    for copy in shares:
        copy.start()
    for copy in shares:
        copy.wait()
    total = sums[0]
    for i in range(1, 2 * count):
        total = total + sums[i]
    shared[...] = lax.rsqrt(total / (HEADS * HD) + 1e-06)

    @pl.loop(0, tiles)
    def _(t):
        at = pl.ds(pl.multiple_of(t * tile, tile), tile)
        for c in range(2):
            factor = jnp.transpose(jnp.broadcast_to(shared[pl.ds(c * tiles + t, 1), :], (HD, tile)))
            for k in range(3):
                lanes = slice(k * HD, (k + 1) * HD)
                normed = (projected[c, at, lanes] * factor * gain_ref[c : c + 1, lanes]).astype(jnp.bfloat16)
                if k < 2:
                    fresh_ref[c, at, lanes] = normed
                else:
                    mine_mid[c, at, :] = normed

    swap = remote(mine_mid, theirs_mid, mid_sem.at[0], mid_sem.at[1], partner)
    swap.start()

    passes = []
    for slot, to, owner in far:
        remote(*middle_copy(to), kv_send.at[2 * slot], kv_recv.at[2 * slot], {"seq": to}).wait_recv()
        spot = middle_slot(owner, x)
        copy = remote(spot, spot, pass_send.at[slot], pass_recv.at[slot], partner)
        copy.start()
        passes.append(copy)

    swap.wait()

    @pl.loop(0, tiles)
    def _(t):
        at = pl.ds(pl.multiple_of(t * tile, tile), tile)
        for c in range(3):
            fresh_ref[c, at, 2 * HD : 3 * HD] = mine_mid[c, at, :] + theirs_mid[c, at, :]

    def sent(owner, sem, where):
        relay(owner, core, sem, where).wait_send()

    for d in range(line):
        @pl.when(jnp.logical_and(z < line - 1, z - d >= 0))
        def _():
            sent(me, up_sem.at[d], above)

        @pl.when(jnp.logical_and(z > 0, z + d < line))
        def _():
            sent(me, down_sem.at[d], below)

    for d in range(1 - line, line):
        @pl.when(jnp.logical_and(z + d >= 0, z + d < line))
        def _():
            sent(me, side_sem.at[line - 1 + d], partner)
            if d:
                sent(me, core_sem.at[line - 1 + d], other)
            sent(me, core_sem.at[2 * line - 1 + line - 1 + d], other)

    for copy in locals_:
        copy.wait()
    for i, copy in enumerate(sends):
        copy.wait_send()
        if i >= len(far):
            copy.wait_recv()
    for copy in passes:
        copy.wait()


def exchange(hidden_rows, weights, gains, kv_cache, count):
    rows, width = hidden_rows.shape
    line = count // PAIR
    total = rows * count
    tiles = total // (2 * HD)
    dma = pltpu.SemaphoreType.DMA
    whole = pl.BlockSpec(memory_space=pl.ANY)
    vmem = pl.BlockSpec(memory_space=pltpu.VMEM)
    return pl.pallas_call(
        functools.partial(exchange_kernel, count),
        out_shape=(
            jax.ShapeDtypeStruct((3, total, 3 * HD), hidden_rows.dtype),
            jax.ShapeDtypeStruct((2, kv_cache.shape[1] * count, 3 * HD), kv_cache.dtype),
        ),
        in_specs=[whole, whole, vmem, whole],
        out_specs=[vmem, vmem],
        scratch_shapes=[
            pltpu.VMEM(kv_cache.shape, jnp.bfloat16),
            pltpu.VMEM((total, width), jnp.bfloat16),
            pltpu.VMEM((6 * HD, width), jnp.bfloat16),
            pltpu.VMEM((3 * HD, width), jnp.bfloat16),
            pltpu.VMEM((2, total, 3 * HD), jnp.float32),
            pltpu.VMEM((2 * tiles, 2 * HD), jnp.float32),
            pltpu.VMEM((3, total, HD), jnp.bfloat16),
            pltpu.VMEM((3, total, HD), jnp.bfloat16),
            pltpu.VMEM((2 * count, 2 * tiles, 2 * HD), jnp.float32),
            dma((2 * count,)), dma((line,)), dma((line,)), dma((2 * line - 1,)),
            dma((2 * (2 * line - 1),)), dma((2 * count,)), dma((2 * count,)), dma((10,)),
            dma((2 * count,)), dma((2 * count,)), dma((count,)), dma((count,)), dma((2,)),
        ],
        compiler_params=pltpu.CompilerParams(
            collective_id=0, has_side_effects=True, vmem_limit_bytes=VMEM_LIMIT
        ),
    )(hidden_rows, weights, gains, kv_cache)


def write_kernel(starts_ref, heads_ref, spread_ref, out_ref, sems):
    copies = [
        pltpu.make_async_copy(
            heads_ref.at[pl.ds(1, 2), pl.ds(number * BLK, BLK), :],
            out_ref.at[:, pl.ds(pl.multiple_of(starts_ref[number], BLK), BLK), :],
            sems.at[number],
        )
        for number in range(NBLK)
    ]
    for copy in copies:
        copy.start()
    for copy in copies:
        copy.wait()


def write_rows(block_starts, heads, spread):
    whole = pl.BlockSpec(memory_space=pl.ANY)
    return pl.pallas_call(
        write_kernel,
        out_shape=jax.ShapeDtypeStruct(spread.shape, spread.dtype),
        in_specs=[pl.BlockSpec(memory_space=pltpu.SMEM), pl.BlockSpec(memory_space=pltpu.VMEM), whole],
        out_specs=whole,
        scratch_shapes=[pltpu.SemaphoreType.DMA((NBLK,))],
        input_output_aliases={2: 0},
        compiler_params=pltpu.CompilerParams(vmem_limit_bytes=VMEM_LIMIT),
    )(block_starts, heads, spread)


UNITS = 5


def finish_kernel(
    count, heads_ref, spread_ref, w_ref, out_ref,
    query, cache, weight, full, total, give, got,
    load_sem, recv_sem, up_sem, down_sem, side_sem, core_sem,
):
    me = lax.axis_index("seq")
    core = lax.axis_index("head")
    line = count // PAIR
    z, x = me // PAIR, me % PAIR
    rows = full.shape[0]
    low = rows // 2
    group = full.shape[1] // line
    above, below = {"seq": me + PAIR}, {"seq": me - PAIR}
    partner = {"seq": z * PAIR + 1 - x}
    other = {"head": 1 - core}

    loads = [pltpu.make_async_copy(heads_ref.at[0], query, load_sem.at[0])]
    for head in range(3):
        lanes = pl.ds(head * HD, HD)
        loads.append(pltpu.make_async_copy(spread_ref.at[:, :, lanes], cache.at[:, :, lanes], load_sem.at[1 + head]))
    loads.append(pltpu.make_async_copy(w_ref, weight, load_sem.at[4]))
    for copy in loads:
        copy.start()

    barrier = pltpu.get_barrier_semaphore()

    def greet(where):
        pl.semaphore_signal(barrier, inc=1, device_id=where, device_id_type=MESH)

    @pl.when(z < line - 1)
    def _():
        greet(above)

    @pl.when(z > 0)
    def _():
        greet(below)

    greet(partner)
    greet(other)
    neighbours = 2 + (z < line - 1).astype(jnp.int32) + (z > 0).astype(jnp.int32)
    pl.semaphore_wait(barrier, neighbours)

    def corner(owner, unit):
        to_z, to_x = owner // PAIR, owner % PAIR
        if unit == UNITS - 1:
            return to_x * low, to_z * group + 2 * HD
        return (unit % 2) * low, to_z * group + to_x * 3 * HD + (unit // 2) * HD

    def spot(owner, unit):
        down, along = corner(owner, unit)
        return full.at[pl.ds(pl.multiple_of(down, low), low), pl.ds(pl.multiple_of(along, HD), HD)]

    def relay(owner, unit, sem, at, where):
        place = spot(owner, unit)
        return remote(place, place, sem.at[UNITS * at + unit], recv_sem.at[UNITS * owner + unit], where)

    def arrived(owner, unit):
        relay(owner, unit, side_sem, 0, partner).wait_recv()

    def attend(unit):
        head = unit // 2
        if unit % 2 == 0:
            loads[1 + head].wait()
        down, along = corner(me, unit)
        lanes = slice(head * HD, (head + 1) * HD)

        @pl.loop(0, low // TILE)
        def _(t):
            at = pl.ds(pl.multiple_of(down + t * TILE, TILE), TILE)
            scores = lax.dot_general(
                query[at, lanes], cache[0, :, lanes], (((1,), (1,)), ((), ())), preferred_element_type=jnp.float32
            )
            top = jnp.max(scores, axis=1, keepdims=True)
            weights = jnp.exp((scores - top) * HD ** (-0.5))
            mass = jnp.sum(weights, axis=1, keepdims=True)
            summed = jnp.dot(weights.astype(jnp.bfloat16), cache[1, :, lanes], preferred_element_type=jnp.float32)
            full[at, pl.ds(pl.multiple_of(along, HD), HD)] = (summed / mass).astype(jnp.bfloat16)

    def send_own(unit):
        @pl.when(z < line - 1)
        def _():
            relay(me, unit, up_sem, 0, above).start()

        @pl.when(z > 0)
        def _():
            relay(me, unit, down_sem, 0, below).start()

        relay(me, unit, side_sem, line - 1, partner).start()

    def handle(unit, d):
        @pl.when(z - d >= 0)
        def _():
            owner = me - d * PAIR
            arrived(owner, unit)

            @pl.when(z < line - 1)
            def _():
                relay(owner, unit, up_sem, d, above).start()

            relay(owner, unit, side_sem, line - 1 - d, partner).start()

        @pl.when(z + d < line)
        def _():
            owner = me + d * PAIR
            arrived(owner, unit)

            @pl.when(z > 0)
            def _():
                relay(owner, unit, down_sem, d, below).start()

            relay(owner, unit, side_sem, line - 1 + d, partner).start()

    def multiply(d):
        @pl.when(jnp.logical_and(z + d >= 0, z + d < line))
        def _():
            for unit in range(UNITS):
                arrived((z + d) * PAIR + 1 - x, unit)
            along = pl.ds(pl.multiple_of((z + d) * group, group), group)

            @pl.loop(0, rows // TILE)
            def _(t):
                at = pl.ds(pl.multiple_of(t * TILE, TILE), TILE)
                part = jnp.dot(full[at, along], weight[along, :], preferred_element_type=jnp.float32)
                if d == 0:
                    total[at, :] = part
                else:
                    total[at, :] = total[at, :] + part

    loads[0].wait()
    for stage in range(UNITS + line - 1):
        if stage < UNITS:
            attend(stage)
            send_own(stage)
        for d in range(1, line):
            if 0 <= stage - d < UNITS:
                handle(stage - d, d)
        d = stage - UNITS
        if d == 0:
            loads[4].wait()
            multiply(0)
        elif d > 0:
            multiply(-d)
            multiply(d)
    multiply(1 - line)
    multiply(line - 1)

    theirs = pl.ds(pl.multiple_of((1 - core) * low, low), low)
    ours = pl.ds(pl.multiple_of(core * low, low), low)
    give[...] = total[theirs, :].astype(jnp.bfloat16)
    swap = remote(give, got, core_sem.at[0], core_sem.at[1], other)
    swap.start()

    for unit in range(UNITS):
        for d in range(line):
            @pl.when(jnp.logical_and(z < line - 1, z - d >= 0))
            def _():
                relay(me, unit, up_sem, d, above).wait_send()

            @pl.when(jnp.logical_and(z > 0, z + d < line))
            def _():
                relay(me, unit, down_sem, d, below).wait_send()

        for d in range(1 - line, line):
            @pl.when(jnp.logical_and(z + d >= 0, z + d < line))
            def _():
                relay(me, unit, side_sem, line - 1 + d, partner).wait_send()

    swap.wait()
    out_ref[...] = (total[ours, :] + got[...].astype(jnp.float32)).astype(jnp.bfloat16)


def finish(heads, spread, w_out, count):
    rows = heads.shape[1]
    features, width = w_out.shape
    line = count // PAIR
    dma = pltpu.SemaphoreType.DMA
    whole = pl.BlockSpec(memory_space=pl.ANY)
    return pl.pallas_call(
        functools.partial(finish_kernel, count),
        out_shape=jax.ShapeDtypeStruct((rows // 2, width), w_out.dtype),
        in_specs=[whole] * 3,
        out_specs=pl.BlockSpec(memory_space=pltpu.VMEM),
        scratch_shapes=[
            pltpu.VMEM(heads.shape[1:], jnp.bfloat16),
            pltpu.VMEM(spread.shape, jnp.bfloat16),
            pltpu.VMEM(w_out.shape, jnp.bfloat16),
            pltpu.VMEM((rows, features), jnp.bfloat16),
            pltpu.VMEM((rows, width), jnp.float32),
            pltpu.VMEM((rows // 2, width), jnp.bfloat16),
            pltpu.VMEM((rows // 2, width), jnp.bfloat16),
            dma((5,)), dma((UNITS * count,)), dma((UNITS * line,)), dma((UNITS * line,)),
            dma((UNITS * (2 * line - 1),)), dma((2,)),
        ],
        compiler_params=pltpu.CompilerParams(
            collective_id=1, has_side_effects=True, vmem_limit_bytes=VMEM_LIMIT
        ),
    )(heads, spread, w_out)


def by_heads(hidden_rows, block_starts, w_qkv, qk_gain, kv_cache, w_out):
    count = lax.axis_size("seq")
    side = lax.axis_index("seq") % PAIR
    columns = w_qkv.shape[2]
    weights = jnp.transpose(w_qkv, (1, 2, 0)).reshape(3 * columns, w_qkv.shape[0])
    part = columns - 2 * HD
    blank = jnp.zeros((2, part), qk_gain.dtype)
    gains = jnp.where(
        side == 0,
        jnp.concatenate([qk_gain, blank], axis=1),
        jnp.concatenate([qk_gain[:, part:], blank, qk_gain[:, :part]], axis=1),
    )
    heads, spread = exchange(hidden_rows, weights, gains, kv_cache, count)
    spread = write_rows(block_starts, heads, spread)
    return finish(heads, spread, w_out, count)


def shifted(block, axis, distance):
    devices = range(lax.axis_size(axis))
    route = [((i - distance) % len(devices), i) for i in devices]
    return lax.ppermute(block, axis, route)


def write_blocks(kv_cache, newer, block_starts):
    length = kv_cache.shape[1]
    first = lax.axis_index("seq") * length
    cache = kv_cache
    for number in range(NBLK):
        offset = block_starts[number] - first
        inside = jnp.logical_and(offset >= 0, offset < length)
        place = jnp.clip(offset, 0, length - BLK)
        block = jnp.transpose(newer[number * BLK : (number + 1) * BLK], (1, 0, 2))
        present = lax.dynamic_slice_in_dim(cache, place, BLK, 1)
        cache = lax.dynamic_update_slice_in_dim(cache, jnp.where(inside, block, present), place, 1)
    return cache


def by_positions(hidden_rows, block_starts, w_qkv, qk_gain, kv_cache, w_out):
    columns = w_qkv.shape[2]
    flat_w = w_qkv.reshape(w_qkv.shape[0], 3 * columns)
    piece = lax.all_gather(hidden_rows, "seq", axis=0, tiled=True)
    projected = jnp.dot(piece, flat_w, preferred_element_type=jnp.float32).reshape(
        piece.shape[0], 3, columns
    )
    paired = projected[:, :2]
    squares = jnp.sum(paired * paired, axis=2)
    totals = lax.psum(squares, ("head", "seq"))
    factor = lax.rsqrt(totals / (HEADS * HD) + 1e-06)
    normed = paired * factor[:, :, None] * qk_gain[None]
    fresh = jnp.concatenate([normed, projected[:, 2:]], axis=1).astype(jnp.bfloat16)
    features = kv_cache.shape[2]
    heads = features // HD
    length = kv_cache.shape[1]
    own = lax.all_to_all(fresh, "seq", split_axis=0, concat_axis=2, tiled=True)
    newer = lax.all_gather(own[:, 1:], "seq", axis=0, tiled=True)
    cache = write_blocks(kv_cache, newer, block_starts)
    keys = cache[0].reshape(length, heads, HD)
    values = cache[1].reshape(length, heads, HD)
    rows = own.shape[0]
    query_rows = own[:, 0].reshape(rows, heads, HD)
    start_state = (
        query_rows,
        jnp.full((rows, heads), -1e30, jnp.float32),
        jnp.zeros((rows, heads), jnp.float32),
        jnp.zeros((rows, heads, HD), jnp.float32),
    )

    def visit(step, state):
        query_now, top_old, total_old, summed_old = state
        scores = jnp.einsum(
            "rhd,thd->hrt", query_now, keys, preferred_element_type=jnp.float32
        ) * HD ** (-0.5)
        top_new = jnp.maximum(top_old, jnp.max(scores, axis=2).T)
        weights = jnp.exp(scores - top_new.T[:, :, None])
        decay = jnp.exp(top_old - top_new)
        total_new = total_old * decay + jnp.sum(weights, axis=2).T
        summed_new = summed_old * decay[:, :, None] + jnp.einsum(
            "hrt,thd->rhd", weights.astype(jnp.bfloat16), values, preferred_element_type=jnp.float32
        )
        return (
            shifted(query_now, "seq", 1),
            shifted(top_new.astype(jnp.bfloat16), "seq", 1).astype(top_new.dtype),
            shifted(total_new.astype(jnp.bfloat16), "seq", 1).astype(total_new.dtype),
            shifted(summed_new.astype(jnp.bfloat16), "seq", 1).astype(summed_new.dtype),
        )

    final = lax.fori_loop(0, lax.axis_size("seq"), visit, start_state)
    summed = final[3]
    total = final[2]
    attended = (summed / total[:, :, None]).astype(jnp.bfloat16).reshape(summed.shape[0], features)
    gathered = lax.all_gather(attended, "seq", axis=0, tiled=True)
    result = lax.psum_scatter(
        jnp.dot(gathered, w_out, preferred_element_type=jnp.float32).astype(jnp.bfloat16),
        "head",
        scatter_dimension=0,
        tiled=True,
    )
    return result


def solution(mesh):
    count = mesh.shape["seq"]
    split = mesh.shape["head"] * count
    fits = mesh.shape["head"] == 2 and count % PAIR == 0 and HEADS * PAIR == 5 * split
    return jax.shard_map(
        by_heads if fits else by_positions,
        mesh=mesh,
        in_specs=(
            P(("grp", "seq"), None),
            P("grp"),
            P(None, None, ("head", "seq")),
            P(None, ("head", "seq")),
            P(None, ("grp", "seq"), "head"),
            P("head", "seq"),
        ),
        out_specs=P(("grp", "head"), "seq"),
        check_vma=False,
    )
```

```python
import functools

import jax
import jax.numpy as jnp
from jax import lax
from jax.experimental import pallas as pl
from jax.experimental.pallas import tpu as pltpu
from jax.sharding import PartitionSpec as P

HEADS = 40
HD = 128
BLK = 128
NBLK = 8
PAIR = 2
TILE = 256
MESH = pl.DeviceIdType.MESH
VMEM_LIMIT = 56 * 1024 * 1024


def remote(src, dst, send, recv, where):
    return pltpu.make_async_remote_copy(
        src_ref=src, dst_ref=dst, send_sem=send, recv_sem=recv, device_id=where, device_id_type=MESH
    )


def exchange_kernel(
    count, hidden_ref, weight_ref, gain_ref, kv_ref, fresh_ref, spread_ref,
    cache_ref, full, pair_w, middle_w, projected, shared, mine_mid, theirs_mid, sums,
    recv_sem, up_sem, down_sem, side_sem, core_sem, kv_send, kv_recv, own_sem,
    sum_send, sum_recv, pass_send, pass_recv, mid_sem,
):
    me = lax.axis_index("seq")
    core = lax.axis_index("head")
    line = count // PAIR
    z, x = me // PAIR, me % PAIR
    rows = hidden_ref.shape[0]
    half = rows // 2
    length = cache_ref.shape[1]
    group = cache_ref.shape[2] // line
    columns = weight_ref.shape[0] // 3
    own_part = columns - 2 * HD
    above, below = {"seq": me + PAIR}, {"seq": me - PAIR}
    partner_at = z * PAIR + 1 - x
    partner = {"seq": partner_at}
    other = {"head": 1 - core}
    peers = [
        (lax.rem(core + c, 2), lax.rem(me + step, count))
        for c in range(2)
        for step in range(count)
        if c or step
    ]

    barrier = pltpu.get_barrier_semaphore()
    for to_core, to in peers:
        pl.semaphore_signal(barrier, inc=1, device_id={"head": to_core, "seq": to}, device_id_type=MESH)
    pl.semaphore_wait(barrier, 2 * count - 1)

    def place(owner, part):
        return full.at[pl.ds(pl.multiple_of(owner * rows + part * half, half), half), :]

    mine = hidden_ref.at[pl.ds(pl.multiple_of(core * half, half), half), :]

    def relay(owner, part, sem, where, src=None):
        spot = place(owner, part)
        return remote(spot if src is None else src, spot, sem, recv_sem.at[owner * 2 + part], where)

    @pl.when(z < line - 1)
    def _():
        relay(me, core, up_sem.at[0], above, mine).start()

    @pl.when(z > 0)
    def _():
        relay(me, core, down_sem.at[0], below, mine).start()

    relay(me, core, side_sem.at[line - 1], partner, mine).start()
    loads = [
        pltpu.make_async_copy(
            hidden_ref, full.at[pl.ds(pl.multiple_of(me * rows, rows), rows), :], own_sem.at[0]
        )
    ]
    for c in range(3):
        pair_at = pl.multiple_of(c * columns + x * own_part, 16)
        middle_at = pl.multiple_of(c * columns + (1 - x) * 2 * HD, 16)
        into = pl.multiple_of(c * HD + x * own_part, 16)
        away = pl.multiple_of(c * HD + (1 - x) * own_part, 16)
        loads.append(
            pltpu.make_async_copy(
                weight_ref.at[pl.ds(pair_at, 2 * HD), :], pair_w.at[pl.ds(c * 2 * HD, 2 * HD), :], own_sem.at[1 + c]
            )
        )
        loads.append(
            pltpu.make_async_copy(
                weight_ref.at[pl.ds(middle_at, own_part), :], middle_w.at[pl.ds(into, own_part), :], own_sem.at[4 + c]
            )
        )
        middle_w[pl.ds(away, own_part), :] = jnp.zeros((own_part, middle_w.shape[1]), middle_w.dtype)
    stage = pltpu.make_async_copy(kv_ref, cache_ref, own_sem.at[9])
    stage.start()
    for copy in loads:
        copy.start()

    def arrived(owner, part):
        relay(owner, part, core_sem.at[0], other).wait_recv()

    def handle_low(d):
        @pl.when(z - d >= 0)
        def _():
            owner = me - d * PAIR
            arrived(owner, core)

            @pl.when(z < line - 1)
            def _():
                relay(owner, core, up_sem.at[d], above).start()

            relay(owner, core, side_sem.at[line - 1 - d], partner).start()
            relay(owner, core, core_sem.at[line - 1 - d], other).start()

    def handle_high(d):
        @pl.when(z + d < line)
        def _():
            owner = me + d * PAIR
            arrived(owner, core)

            @pl.when(z > 0)
            def _():
                relay(owner, core, down_sem.at[d], below).start()

            relay(owner, core, side_sem.at[line - 1 + d], partner).start()
            relay(owner, core, core_sem.at[line - 1 + d], other).start()

    def handle_side(d):
        @pl.when(jnp.logical_and(z + d >= 0, z + d < line))
        def _():
            owner = (z + d) * PAIR + 1 - x
            arrived(owner, core)
            relay(owner, core, core_sem.at[2 * line - 1 + line - 1 + d], other).start()

    def source(owner):
        return owner // PAIR, owner % PAIR

    def pair_copy(step, to):
        to_z, to_x = source(to)
        at = pl.multiple_of(to_z * group + to_x * 3 * HD, HD)
        src = cache_ref.at[:, :, pl.ds(at, 2 * HD)]
        dst = spread_ref.at[:, pl.ds(pl.multiple_of(me * length, length), length), pl.ds(0, 2 * HD)]
        return src, dst

    part = length // 2

    def middle_slot(owner, which):
        at = pl.multiple_of(owner * length + which * part, part)
        return spread_ref.at[:, pl.ds(at, part), pl.ds(2 * HD, HD)]

    def middle_copy(to):
        to_z, to_x = source(to)
        at = pl.multiple_of(to_z * group + 2 * HD, HD)
        low = pl.multiple_of(to_x * part, part)
        return cache_ref.at[:, pl.ds(low, part), pl.ds(at, HD)], middle_slot(me, to_x)

    middle_at = pl.multiple_of(z * group + 2 * HD, HD)
    whole_middle = (
        cache_ref.at[:, :, pl.ds(middle_at, HD)],
        spread_ref.at[:, pl.ds(pl.multiple_of(me * length, length), length), pl.ds(2 * HD, HD)],
    )
    locals_ = [
        pltpu.make_async_copy(*pair_copy(0, me), own_sem.at[7]),
        pltpu.make_async_copy(*whole_middle, own_sem.at[8]),
    ]
    far = []
    for hop in range(1, line):
        for across in range(PAIR):
            to = lax.rem(z + hop, line) * PAIR + lax.rem(x + across, PAIR)
            far.append((hop * PAIR + across, to, lax.rem(z + line - hop, line) * PAIR + lax.rem(x + across, PAIR)))
    sends = []
    for slot, to, _ in far:
        sends.append(remote(*middle_copy(to), kv_send.at[2 * slot], kv_recv.at[2 * slot], {"seq": to}))
    sends.append(remote(*whole_middle, kv_send.at[0], kv_recv.at[0], partner))
    for slot, to, _ in far:
        sends.append(remote(*pair_copy(slot, to), kv_send.at[2 * slot + 1], kv_recv.at[2 * slot + 1], {"seq": to}))
    sends.append(remote(*pair_copy(0, partner_at), kv_send.at[1], kv_recv.at[1], partner))

    early = len(far) + EARLY
    for d in range(line):
        if d + 1 < line:
            handle_low(d + 1)
            handle_high(d + 1)
        if d + 1 == max(line - 2, 1):
            stage.wait()
            for copy in sends[:early] + locals_:
                copy.start()
        handle_side(d)
        if d:
            handle_side(-d)

    for copy in loads:
        copy.wait()
    for step in range(1, count):
        arrived(lax.rem(me + step, count), 1 - core)

    tile = 2 * HD
    tiles = full.shape[0] // tile
    nt = (((1,), (1,)), ((), ()))

    @pl.loop(0, tiles)
    def _(t):
        at = pl.ds(pl.multiple_of(t * tile, tile), tile)
        lines = full[at, :]
        for c in range(3):
            wide = lax.dot_general(
                lines, pair_w[c * 2 * HD : (c + 1) * 2 * HD, :], nt, preferred_element_type=jnp.float32
            )
            thin = lax.dot_general(
                lines, middle_w[c * HD : (c + 1) * HD, :], nt, preferred_element_type=jnp.float32
            )
            if c == 2:
                fresh_ref[2, at, 0 : 2 * HD] = wide.astype(jnp.bfloat16)
                mine_mid[2, at, :] = thin.astype(jnp.bfloat16)
            else:
                projected[c, at, 0 : 2 * HD] = wide
                projected[c, at, 2 * HD : 3 * HD] = thin
                mine_mid[c, at, :] = (thin * gain_ref[c : c + 1, 2 * HD : 3 * HD]).astype(jnp.bfloat16)
                square = jnp.sum(wide * wide, axis=1, keepdims=True) + jnp.sum(thin * thin, axis=1, keepdims=True)
                turned = jnp.transpose(jnp.broadcast_to(square, (tile, HD)))
                sums[0, pl.ds(c * tiles + t, 1), :] = turned[0:1, :]

    shares = []
    for i, (to_core, to) in enumerate(peers):
        shares.append(
            remote(
                sums.at[0], sums.at[i + 1], sum_send.at[i], sum_recv.at[i], {"head": to_core, "seq": to}
            )
        )
    for copy in shares:
        copy.start()
    swap = remote(mine_mid, theirs_mid, mid_sem.at[0], mid_sem.at[1], partner)
    swap.start()
    for copy in sends[early:]:
        copy.start()

    passes = []
    for slot, to, owner in far:
        remote(*middle_copy(to), kv_send.at[2 * slot], kv_recv.at[2 * slot], {"seq": to}).wait_recv()
        spot = middle_slot(owner, x)
        copy = remote(spot, spot, pass_send.at[slot], pass_recv.at[slot], partner)
        copy.start()
        passes.append(copy)

    for copy in shares:
        copy.wait()
    total = sums[0]
    for i in range(1, 2 * count):
        total = total + sums[i]
    shared[...] = lax.rsqrt(total / (HEADS * HD) + 1e-06)

    swap.wait()

    @pl.loop(0, tiles)
    def _(t):
        at = pl.ds(pl.multiple_of(t * tile, tile), tile)
        for c in range(2):
            factor = jnp.transpose(jnp.broadcast_to(shared[pl.ds(c * tiles + t, 1), :], (HD, tile)))
            for k in range(3):
                lanes = slice(k * HD, (k + 1) * HD)
                normed = projected[c, at, lanes] * factor * gain_ref[c : c + 1, lanes]
                if k == 2:
                    normed = normed + theirs_mid[c, at, :].astype(jnp.float32) * factor
                fresh_ref[c, at, lanes] = normed.astype(jnp.bfloat16)
        fresh_ref[2, at, 2 * HD : 3 * HD] = mine_mid[2, at, :] + theirs_mid[2, at, :]

    def sent(owner, sem, where):
        relay(owner, core, sem, where).wait_send()

    for d in range(line):
        @pl.when(jnp.logical_and(z < line - 1, z - d >= 0))
        def _():
            sent(me, up_sem.at[d], above)

        @pl.when(jnp.logical_and(z > 0, z + d < line))
        def _():
            sent(me, down_sem.at[d], below)

    for d in range(1 - line, line):
        @pl.when(jnp.logical_and(z + d >= 0, z + d < line))
        def _():
            sent(me, side_sem.at[line - 1 + d], partner)
            if d:
                sent(me, core_sem.at[line - 1 + d], other)
            sent(me, core_sem.at[2 * line - 1 + line - 1 + d], other)

    for copy in locals_:
        copy.wait()
    for i, copy in enumerate(sends):
        copy.wait_send()
        if i >= len(far):
            copy.wait_recv()
    for copy in passes:
        copy.wait()


def exchange(hidden_rows, weights, gains, kv_cache, count):
    rows, width = hidden_rows.shape
    line = count // PAIR
    total = rows * count
    tiles = total // (2 * HD)
    dma = pltpu.SemaphoreType.DMA
    whole = pl.BlockSpec(memory_space=pl.ANY)
    vmem = pl.BlockSpec(memory_space=pltpu.VMEM)
    return pl.pallas_call(
        functools.partial(exchange_kernel, count),
        out_shape=(
            jax.ShapeDtypeStruct((3, total, 3 * HD), hidden_rows.dtype),
            jax.ShapeDtypeStruct((2, kv_cache.shape[1] * count, 3 * HD), kv_cache.dtype),
        ),
        in_specs=[whole, whole, vmem, whole],
        out_specs=[vmem, vmem],
        scratch_shapes=[
            pltpu.VMEM(kv_cache.shape, jnp.bfloat16),
            pltpu.VMEM((total, width), jnp.bfloat16),
            pltpu.VMEM((6 * HD, width), jnp.bfloat16),
            pltpu.VMEM((3 * HD, width), jnp.bfloat16),
            pltpu.VMEM((2, total, 3 * HD), jnp.float32),
            pltpu.VMEM((2 * tiles, 2 * HD), jnp.float32),
            pltpu.VMEM((3, total, HD), jnp.bfloat16),
            pltpu.VMEM((3, total, HD), jnp.bfloat16),
            pltpu.VMEM((2 * count, 2 * tiles, 2 * HD), jnp.float32),
            dma((2 * count,)), dma((line,)), dma((line,)), dma((2 * line - 1,)),
            dma((2 * (2 * line - 1),)), dma((2 * count,)), dma((2 * count,)), dma((10,)),
            dma((2 * count,)), dma((2 * count,)), dma((count,)), dma((count,)), dma((2,)),
        ],
        compiler_params=pltpu.CompilerParams(
            collective_id=0, has_side_effects=True, vmem_limit_bytes=VMEM_LIMIT
        ),
    )(hidden_rows, weights, gains, kv_cache)


def write_kernel(starts_ref, heads_ref, spread_ref, out_ref, sems):
    copies = [
        pltpu.make_async_copy(
            heads_ref.at[pl.ds(1, 2), pl.ds(number * BLK, BLK), :],
            out_ref.at[:, pl.ds(pl.multiple_of(starts_ref[number], BLK), BLK), :],
            sems.at[number],
        )
        for number in range(NBLK)
    ]
    for copy in copies:
        copy.start()
    for copy in copies:
        copy.wait()


def write_rows(block_starts, heads, spread):
    whole = pl.BlockSpec(memory_space=pl.ANY)
    return pl.pallas_call(
        write_kernel,
        out_shape=jax.ShapeDtypeStruct(spread.shape, spread.dtype),
        in_specs=[pl.BlockSpec(memory_space=pltpu.SMEM), pl.BlockSpec(memory_space=pltpu.VMEM), whole],
        out_specs=whole,
        scratch_shapes=[pltpu.SemaphoreType.DMA((NBLK,))],
        input_output_aliases={2: 0},
        compiler_params=pltpu.CompilerParams(vmem_limit_bytes=VMEM_LIMIT),
    )(block_starts, heads, spread)


UNITS = 5
EARLY = 3


def finish_kernel(
    count, heads_ref, spread_ref, w_ref, out_ref,
    query, cache, weight, full, total, give, got,
    load_sem, recv_sem, up_sem, down_sem, side_sem, core_sem,
):
    me = lax.axis_index("seq")
    core = lax.axis_index("head")
    line = count // PAIR
    z, x = me // PAIR, me % PAIR
    rows = full.shape[0]
    low = rows // 2
    group = full.shape[1] // line
    above, below = {"seq": me + PAIR}, {"seq": me - PAIR}
    partner = {"seq": z * PAIR + 1 - x}
    other = {"head": 1 - core}

    loads = [pltpu.make_async_copy(heads_ref.at[0], query, load_sem.at[0])]
    for head in range(3):
        lanes = pl.ds(head * HD, HD)
        loads.append(pltpu.make_async_copy(spread_ref.at[:, :, lanes], cache.at[:, :, lanes], load_sem.at[1 + head]))
    loads.append(pltpu.make_async_copy(w_ref, weight, load_sem.at[4]))
    for copy in loads:
        copy.start()

    barrier = pltpu.get_barrier_semaphore()

    def greet(where):
        pl.semaphore_signal(barrier, inc=1, device_id=where, device_id_type=MESH)

    @pl.when(z < line - 1)
    def _():
        greet(above)

    @pl.when(z > 0)
    def _():
        greet(below)

    greet(partner)
    greet(other)
    neighbours = 2 + (z < line - 1).astype(jnp.int32) + (z > 0).astype(jnp.int32)
    pl.semaphore_wait(barrier, neighbours)

    def corner(owner, unit):
        to_z, to_x = owner // PAIR, owner % PAIR
        if unit == UNITS - 1:
            return to_x * low, to_z * group + 2 * HD
        return (unit % 2) * low, to_z * group + to_x * 3 * HD + (unit // 2) * HD

    def spot(owner, unit):
        down, along = corner(owner, unit)
        return full.at[pl.ds(pl.multiple_of(down, low), low), pl.ds(pl.multiple_of(along, HD), HD)]

    def relay(owner, unit, sem, at, where):
        place = spot(owner, unit)
        return remote(place, place, sem.at[UNITS * at + unit], recv_sem.at[UNITS * owner + unit], where)

    def arrived(owner, unit):
        relay(owner, unit, side_sem, 0, partner).wait_recv()

    def attend(unit):
        head = unit // 2
        if unit % 2 == 0:
            loads[1 + head].wait()
        down, along = corner(me, unit)
        lanes = slice(head * HD, (head + 1) * HD)

        @pl.loop(0, low // TILE)
        def _(t):
            at = pl.ds(pl.multiple_of(down + t * TILE, TILE), TILE)
            scores = lax.dot_general(
                query[at, lanes], cache[0, :, lanes], (((1,), (1,)), ((), ())), preferred_element_type=jnp.float32
            )
            top = jnp.max(scores, axis=1, keepdims=True)
            weights = jnp.exp((scores - top) * HD ** (-0.5))
            mass = jnp.sum(weights, axis=1, keepdims=True)
            summed = jnp.dot(weights.astype(jnp.bfloat16), cache[1, :, lanes], preferred_element_type=jnp.float32)
            full[at, pl.ds(pl.multiple_of(along, HD), HD)] = (summed / mass).astype(jnp.bfloat16)

    def send_own(unit):
        @pl.when(z < line - 1)
        def _():
            relay(me, unit, up_sem, 0, above).start()

        @pl.when(z > 0)
        def _():
            relay(me, unit, down_sem, 0, below).start()

        relay(me, unit, side_sem, line - 1, partner).start()

    def handle(unit, d):
        @pl.when(z - d >= 0)
        def _():
            owner = me - d * PAIR
            arrived(owner, unit)

            @pl.when(z < line - 1)
            def _():
                relay(owner, unit, up_sem, d, above).start()

            relay(owner, unit, side_sem, line - 1 - d, partner).start()

        @pl.when(z + d < line)
        def _():
            owner = me + d * PAIR
            arrived(owner, unit)

            @pl.when(z > 0)
            def _():
                relay(owner, unit, down_sem, d, below).start()

            relay(owner, unit, side_sem, line - 1 + d, partner).start()

    def multiply(d):
        @pl.when(jnp.logical_and(z + d >= 0, z + d < line))
        def _():
            for unit in range(UNITS):
                arrived((z + d) * PAIR + 1 - x, unit)
            along = pl.ds(pl.multiple_of((z + d) * group, group), group)

            @pl.loop(0, rows // TILE)
            def _(t):
                at = pl.ds(pl.multiple_of(t * TILE, TILE), TILE)
                part = jnp.dot(full[at, along], weight[along, :], preferred_element_type=jnp.float32)
                if d == 0:
                    total[at, :] = part
                else:
                    total[at, :] = total[at, :] + part

    loads[0].wait()
    for stage in range(UNITS + line - 1):
        if stage < UNITS:
            attend(stage)
            send_own(stage)
        for d in range(1, line):
            if 0 <= stage - d < UNITS:
                handle(stage - d, d)
        d = stage - UNITS
        if d == 0:
            loads[4].wait()
            multiply(0)
        elif d > 0:
            multiply(-d)
            multiply(d)
    multiply(1 - line)
    multiply(line - 1)

    theirs = pl.ds(pl.multiple_of((1 - core) * low, low), low)
    ours = pl.ds(pl.multiple_of(core * low, low), low)
    give[...] = total[theirs, :].astype(jnp.bfloat16)
    swap = remote(give, got, core_sem.at[0], core_sem.at[1], other)
    swap.start()

    for unit in range(UNITS):
        for d in range(line):
            @pl.when(jnp.logical_and(z < line - 1, z - d >= 0))
            def _():
                relay(me, unit, up_sem, d, above).wait_send()

            @pl.when(jnp.logical_and(z > 0, z + d < line))
            def _():
                relay(me, unit, down_sem, d, below).wait_send()

        for d in range(1 - line, line):
            @pl.when(jnp.logical_and(z + d >= 0, z + d < line))
            def _():
                relay(me, unit, side_sem, line - 1 + d, partner).wait_send()

    swap.wait()
    out_ref[...] = (total[ours, :] + got[...].astype(jnp.float32)).astype(jnp.bfloat16)


def finish(heads, spread, w_out, count):
    rows = heads.shape[1]
    features, width = w_out.shape
    line = count // PAIR
    dma = pltpu.SemaphoreType.DMA
    whole = pl.BlockSpec(memory_space=pl.ANY)
    return pl.pallas_call(
        functools.partial(finish_kernel, count),
        out_shape=jax.ShapeDtypeStruct((rows // 2, width), w_out.dtype),
        in_specs=[whole] * 3,
        out_specs=pl.BlockSpec(memory_space=pltpu.VMEM),
        scratch_shapes=[
            pltpu.VMEM(heads.shape[1:], jnp.bfloat16),
            pltpu.VMEM(spread.shape, jnp.bfloat16),
            pltpu.VMEM(w_out.shape, jnp.bfloat16),
            pltpu.VMEM((rows, features), jnp.bfloat16),
            pltpu.VMEM((rows, width), jnp.float32),
            pltpu.VMEM((rows // 2, width), jnp.bfloat16),
            pltpu.VMEM((rows // 2, width), jnp.bfloat16),
            dma((5,)), dma((UNITS * count,)), dma((UNITS * line,)), dma((UNITS * line,)),
            dma((UNITS * (2 * line - 1),)), dma((2,)),
        ],
        compiler_params=pltpu.CompilerParams(
            collective_id=1, has_side_effects=True, vmem_limit_bytes=VMEM_LIMIT
        ),
    )(heads, spread, w_out)


def by_heads(hidden_rows, block_starts, w_qkv, qk_gain, kv_cache, w_out):
    count = lax.axis_size("seq")
    side = lax.axis_index("seq") % PAIR
    columns = w_qkv.shape[2]
    weights = jnp.transpose(w_qkv, (1, 2, 0)).reshape(3 * columns, w_qkv.shape[0])
    part = columns - 2 * HD
    blank = jnp.zeros((2, part), qk_gain.dtype)
    gains = jnp.where(
        side == 0,
        jnp.concatenate([qk_gain, blank], axis=1),
        jnp.concatenate([qk_gain[:, part:], blank, qk_gain[:, :part]], axis=1),
    )
    heads, spread = exchange(hidden_rows, weights, gains, kv_cache, count)
    spread = write_rows(block_starts, heads, spread)
    return finish(heads, spread, w_out, count)


def shifted(block, axis, distance):
    devices = range(lax.axis_size(axis))
    route = [((i - distance) % len(devices), i) for i in devices]
    return lax.ppermute(block, axis, route)


def write_blocks(kv_cache, newer, block_starts):
    length = kv_cache.shape[1]
    first = lax.axis_index("seq") * length
    cache = kv_cache
    for number in range(NBLK):
        offset = block_starts[number] - first
        inside = jnp.logical_and(offset >= 0, offset < length)
        place = jnp.clip(offset, 0, length - BLK)
        block = jnp.transpose(newer[number * BLK : (number + 1) * BLK], (1, 0, 2))
        present = lax.dynamic_slice_in_dim(cache, place, BLK, 1)
        cache = lax.dynamic_update_slice_in_dim(cache, jnp.where(inside, block, present), place, 1)
    return cache


def by_positions(hidden_rows, block_starts, w_qkv, qk_gain, kv_cache, w_out):
    columns = w_qkv.shape[2]
    flat_w = w_qkv.reshape(w_qkv.shape[0], 3 * columns)
    piece = lax.all_gather(hidden_rows, "seq", axis=0, tiled=True)
    projected = jnp.dot(piece, flat_w, preferred_element_type=jnp.float32).reshape(
        piece.shape[0], 3, columns
    )
    paired = projected[:, :2]
    squares = jnp.sum(paired * paired, axis=2)
    totals = lax.psum(squares, ("head", "seq"))
    factor = lax.rsqrt(totals / (HEADS * HD) + 1e-06)
    normed = paired * factor[:, :, None] * qk_gain[None]
    fresh = jnp.concatenate([normed, projected[:, 2:]], axis=1).astype(jnp.bfloat16)
    features = kv_cache.shape[2]
    heads = features // HD
    length = kv_cache.shape[1]
    own = lax.all_to_all(fresh, "seq", split_axis=0, concat_axis=2, tiled=True)
    newer = lax.all_gather(own[:, 1:], "seq", axis=0, tiled=True)
    cache = write_blocks(kv_cache, newer, block_starts)
    keys = cache[0].reshape(length, heads, HD)
    values = cache[1].reshape(length, heads, HD)
    rows = own.shape[0]
    query_rows = own[:, 0].reshape(rows, heads, HD)
    start_state = (
        query_rows,
        jnp.full((rows, heads), -1e30, jnp.float32),
        jnp.zeros((rows, heads), jnp.float32),
        jnp.zeros((rows, heads, HD), jnp.float32),
    )

    def visit(step, state):
        query_now, top_old, total_old, summed_old = state
        scores = jnp.einsum(
            "rhd,thd->hrt", query_now, keys, preferred_element_type=jnp.float32
        ) * HD ** (-0.5)
        top_new = jnp.maximum(top_old, jnp.max(scores, axis=2).T)
        weights = jnp.exp(scores - top_new.T[:, :, None])
        decay = jnp.exp(top_old - top_new)
        total_new = total_old * decay + jnp.sum(weights, axis=2).T
        summed_new = summed_old * decay[:, :, None] + jnp.einsum(
            "hrt,thd->rhd", weights.astype(jnp.bfloat16), values, preferred_element_type=jnp.float32
        )
        return (
            shifted(query_now, "seq", 1),
            shifted(top_new.astype(jnp.bfloat16), "seq", 1).astype(top_new.dtype),
            shifted(total_new.astype(jnp.bfloat16), "seq", 1).astype(total_new.dtype),
            shifted(summed_new.astype(jnp.bfloat16), "seq", 1).astype(summed_new.dtype),
        )

    final = lax.fori_loop(0, lax.axis_size("seq"), visit, start_state)
    summed = final[3]
    total = final[2]
    attended = (summed / total[:, :, None]).astype(jnp.bfloat16).reshape(summed.shape[0], features)
    gathered = lax.all_gather(attended, "seq", axis=0, tiled=True)
    result = lax.psum_scatter(
        jnp.dot(gathered, w_out, preferred_element_type=jnp.float32).astype(jnp.bfloat16),
        "head",
        scatter_dimension=0,
        tiled=True,
    )
    return result


def solution(mesh):
    count = mesh.shape["seq"]
    split = mesh.shape["head"] * count
    fits = mesh.shape["head"] == 2 and count % PAIR == 0 and HEADS * PAIR == 5 * split
    return jax.shard_map(
        by_heads if fits else by_positions,
        mesh=mesh,
        in_specs=(
            P(("grp", "seq"), None),
            P("grp"),
            P(None, None, ("head", "seq")),
            P(None, ("head", "seq")),
            P(None, ("grp", "seq"), "head"),
            P("head", "seq"),
        ),
        out_specs=P(("grp", "head"), "seq"),
        check_vma=False,
    )
```
